256 devices in a mesh: dp: 16 (over x, y), mp: 16 (over z, core).
Axes of the slice: x: 4, y: 4, z: 8, core: 2. Of those that a mesh axis runs over, the one named last changes fastest.
Arguments:
- hidden_in: bfloat16 [2048, 8192], P('dp', 'mp'), may hold values from -256 to 256
- out_grad: bfloat16 [2048, 8192], P('dp', 'mp'), may hold values from -1.796875 to 1.796875
- neighbours: bfloat16 [512, 128, 1536], P('dp', 'mp'), may hold values from -6 to 6
- counts: int32 [32], P('dp'), may hold values from 2 to 10, as said below
- slot_owner: int32 [512], P('dp'), may hold values from -1 to 319, as said below
- w_query: bfloat16 [8192, 4096], P(None, 'mp'), may hold values from -0.0625 to 0.0625
- w_key: bfloat16 [1536, 4096], P(None, 'mp'), may hold values from -0.15625 to 0.15625
- w_value: bfloat16 [1536, 4096], P(None, 'mp'), may hold values from -0.15625 to 0.15625
- w_out: bfloat16 [4096, 8192], P('mp'), may hold values from -0.59765625 to 0.59765625
Outputs:
- layer_out: bfloat16 [2048, 8192], P('dp', 'mp')
- neighbour_grad: bfloat16 [512, 128, 1536], P('dp', 'mp')
The draws below stay inside these ranges and needn't reach their ends.
Inputs may be any that keep to these rules, and one draw needn't show every extreme that they name: `counts`: every draw has one decoder group (spans g * 2 to g * 2 + 1) whose spans all have 10 neighbours. `slot_owner`: entry i is the span slot c * 10 + j that encoder slot i fills, or -1 for an empty encoder slot. Each slot with j < counts[c] is named exactly once, no other slot is named. The 32 entries of one index of dp name at most 2 slots of the spans of one decoder group (spans g * 2 to g * 2 + 1), and in every draw some index of dp names exactly 2 for some group.
All inputs are finite; a program needn't handle non-finite values.
Results may differ from the reference program's by a relative error of at most 0.024.
Values may be sent and summed in bfloat16 or wider, within the bound.
No kernel may reach another device: no remote copies, remote signals or barrier semaphores. Data moves between devices by JAX's collectives and lax.ppermute only.
A program may use at most 128 MiB of HBM per device.

```python
import math
import jax
import jax.numpy as jnp
from jax import lax

D = 8192
HEADS = 32
DH = 128
ENC = 1536
CLEN = 64
NLEN = 128
MAXN = 10
CH = 2
QW = 4096
NCH = 32
TOKENS = 2048
NEIGH = 512
N_MP = 16


def shuffled(sub_key, length):
    return jax.random.permutation(sub_key, length)


def neighbour_plan(key):
    key_count, key_group, key_source, key_shuffle = jax.random.split(key, 4)
    groups = NCH // CH
    capacity = (CH * MAXN + groups - 1) // groups
    counts = jax.random.randint(key_count, (NCH,), 2, MAXN + 1)
    full_group = jax.random.randint(key_group, (), 0, groups)
    span_group = jnp.arange(NCH) // CH
    counts = jnp.where(span_group == full_group, MAXN, counts).astype(jnp.int32)
    orders = jax.vmap(partial_perm(groups))(jax.random.split(key_source, groups))
    inverse = jnp.argsort(orders, axis=1)
    place = jnp.transpose(inverse)[:, :, None] * capacity + jnp.arange(capacity)[None, None, :]
    span_in = jnp.minimum(place // MAXN, CH - 1)
    slot_in = place % MAXN
    span_ids = jnp.arange(groups)[None, :, None] * CH + span_in
    valid = (place < CH * MAXN) & (slot_in < counts[span_ids])
    targets = jnp.where(valid, span_ids * MAXN + slot_in, -1).reshape(groups, groups * capacity)
    shuffles = jax.vmap(partial_perm(groups * capacity))(jax.random.split(key_shuffle, groups))
    owners = jnp.take_along_axis(targets, shuffles, axis=1).reshape(-1).astype(jnp.int32)
    return (counts, owners)


def partial_perm(length):

    def apply_perm(sub_key):
        return shuffled(sub_key, length)
    return apply_perm


def draw_counts(key, part):
    return neighbour_plan(key)[0]


def draw_slot_owner(key, part):
    return neighbour_plan(key)[1]


def draw_hidden_in(key, part):
    key = jax.random.fold_in(key, 11)
    key_base = jax.random.fold_in(key, 0)
    values = jnp.clip(jax.random.normal(key_base, (TOKENS, D), jnp.float32), -6.0, 6.0)
    return values.astype(jnp.bfloat16)


def shard_levels(own_key, extent, pieces, low, largest):
    level, own = 1.0, jax.random.fold_in(own_key, 6)
    for dim, shards_of in pieces:
        steps = jnp.exp(jax.random.uniform(jax.random.fold_in(own, dim), (shards_of,), jnp.float32, low / len(pieces), largest / len(pieces)))
        level = level * jnp.repeat(steps, extent[dim] // shards_of).reshape([-1 if axis == dim else 1 for axis in range(len(extent))])
    return level


def centred(key, shape, deviation, most, cuts=(), kind=jnp.bfloat16):
    drawn = jax.random.normal(key, shape, jnp.float32) * deviation
    if len(cuts) > 0:
        drawn = shard_levels(key, shape, cuts, -0.22, 0.18) * drawn
    return jnp.clip(drawn, min=-most, max=most).astype(kind)


def setup_inputs(seed: int = 0) -> dict:
    seeds = jax.random.split(jax.random.key(seed), 10)
    hidden_in = draw_hidden_in(jax.random.fold_in(seeds[9], 71), 0)
    out_grad = centred(seeds[1], (TOKENS, D), 0.3, 1.796875, ((0, 16), (1, 16)))
    neighbours = centred(seeds[2], (NEIGH, NLEN, ENC), 1.0, 6.0, ((0, 16), (1, 16)))
    counts = draw_counts(jax.random.fold_in(seeds[9], 71), 0)
    slot_owner = draw_slot_owner(jax.random.fold_in(seeds[9], 71), 0)
    w_query = centred(seeds[5], (D, QW), D ** -0.5, 0.0625, ((1, 16),))
    w_key = centred(seeds[6], (ENC, QW), ENC ** -0.5, 0.15625, ((1, 16),))
    w_value = centred(seeds[7], (ENC, QW), ENC ** -0.5, 0.15625, ((1, 16),))
    w_out = centred(seeds[8], (QW, D), 0.1, 0.59765625, ((0, 16),))
    return {"hidden_in": hidden_in, "out_grad": out_grad, "neighbours": neighbours, "counts": counts, "slot_owner": slot_owner, "w_query": w_query, "w_key": w_key, "w_value": w_value, "w_out": w_out}


def span_attention(queries, key_rows, value_rows, live_keys, grad_attended):
    score_scale = 1.0 / math.sqrt(DH)
    query_f = queries.astype(jnp.float32)
    key_f = key_rows.astype(jnp.float32)
    value_f = value_rows.astype(jnp.float32)
    grad_f = grad_attended.astype(jnp.float32)
    scores = jnp.einsum('qhd,khd->hqk', query_f, key_f) * score_scale
    scores = jnp.where(live_keys[None, None, :], scores, -jnp.inf)
    peak_score = lax.optimization_barrier(jnp.max(scores, axis=-1, keepdims=True))
    exponent = jnp.exp(scores - peak_score)
    weights = exponent / lax.optimization_barrier(jnp.sum(exponent, axis=-1, keepdims=True))
    weights_bf = weights.astype(jnp.bfloat16).astype(jnp.float32)
    attended = jnp.einsum('hqk,khd->qhd', weights_bf, value_f).astype(jnp.bfloat16)
    grad_values = jnp.einsum('hqk,qhd->khd', weights_bf, grad_f).astype(jnp.bfloat16)
    grad_weights = jnp.einsum('qhd,khd->hqk', grad_f, value_f)
    inner_sum = lax.optimization_barrier(jnp.sum(weights * grad_weights, axis=-1, keepdims=True))
    grad_scores = (weights * (grad_weights - inner_sum) * score_scale).astype(jnp.bfloat16)
    grad_keys = jnp.einsum('hqk,qhd->khd', grad_scores.astype(jnp.float32), query_f).astype(jnp.bfloat16)
    return (attended, grad_keys, grad_values)

def reference(hidden_in, out_grad, neighbours, counts, slot_owner, w_query, w_key, w_value, w_out):
    slot_ids = jnp.arange(NCH * MAXN, dtype=jnp.int32)
    matches = slot_owner[None, :] == slot_ids[:, None]
    encoder_ids = jnp.arange(NEIGH, dtype=jnp.int32)
    source = lax.optimization_barrier(jnp.sum(jnp.where(matches, encoder_ids[None, :], 0), axis=1)).astype(jnp.int32)
    gathered = jnp.take(neighbours, source, axis=0)
    queries = jnp.dot(hidden_in, w_query, preferred_element_type=jnp.float32).astype(jnp.bfloat16)
    grad_attended = lax.dot_general(out_grad, w_out, (((1,), (1,)), ((), ())), preferred_element_type=jnp.float32).astype(jnp.bfloat16)
    group_width = QW // N_MP

    def per_span(inputs):
        span_query, span_grad, span_neigh, span_count = inputs
        flat_rows = span_neigh.reshape(MAXN * NLEN, ENC)
        key_rows = jnp.dot(flat_rows, w_key, preferred_element_type=jnp.float32).astype(jnp.bfloat16)
        value_rows = jnp.dot(flat_rows, w_value, preferred_element_type=jnp.float32).astype(jnp.bfloat16)
        live_keys = jnp.arange(MAXN * NLEN, dtype=jnp.int32) // NLEN < span_count
        attended, grad_keys, grad_values = span_attention(span_query.reshape(CLEN, HEADS, DH), key_rows.reshape(MAXN * NLEN, HEADS, DH), value_rows.reshape(MAXN * NLEN, HEADS, DH), live_keys, span_grad.reshape(CLEN, HEADS, DH))
        grad_keys = grad_keys.reshape(MAXN * NLEN, QW)
        grad_values = grad_values.reshape(MAXN * NLEN, QW)
        running = jnp.zeros((MAXN * NLEN, ENC), jnp.float32)
        for shard in range(N_MP):
            low = shard * group_width
            high = low + group_width
            partial_value = lax.dot_general(grad_keys[:, low:high], w_key[:, low:high], (((1,), (1,)), ((), ())), preferred_element_type=jnp.float32)
            partial_value = partial_value + lax.dot_general(grad_values[:, low:high], w_value[:, low:high], (((1,), (1,)), ((), ())), preferred_element_type=jnp.float32)
            rounded = lax.optimization_barrier(partial_value.astype(jnp.bfloat16))
            running = running + rounded.astype(jnp.float32)
        return (attended.reshape(CLEN, QW), running.astype(jnp.bfloat16).reshape(MAXN, NLEN, ENC))
    attended, grad_slots = lax.map(per_span, (queries.reshape(NCH, CLEN, QW), grad_attended.reshape(NCH, CLEN, QW), gathered.reshape(NCH, MAXN, NLEN, ENC), counts))
    attended = attended.reshape(TOKENS, QW)
    running = jnp.zeros((TOKENS, D), jnp.float32)
    for shard in range(N_MP):
        low = shard * group_width
        high = low + group_width
        partial_value = jnp.dot(attended[:, low:high], w_out[low:high, :], preferred_element_type=jnp.float32)
        rounded = lax.optimization_barrier(partial_value.astype(jnp.bfloat16))
        running = running + rounded.astype(jnp.float32)
    layer_out = running.astype(jnp.bfloat16)
    grad_slots = grad_slots.reshape(NCH * MAXN, NLEN, ENC)
    picked = jnp.take(grad_slots, jnp.maximum(slot_owner, 0).astype(jnp.int32), axis=0)
    neighbour_grad = jnp.where((slot_owner >= 0)[:, None, None], picked, jnp.zeros_like(picked))
    return (layer_out, neighbour_grad)
```

```python
import math

import jax
import jax.numpy as jnp
from jax import lax
from jax.sharding import PartitionSpec as P

DH = 128
MAXN = 10
BF = jnp.bfloat16
F32 = jnp.float32
LAST = (((1,), (1,)), ((), ()))


def dot(a, b):
    return jnp.dot(a, b, preferred_element_type=F32)


def dot_t(a, b):
    return lax.dot_general(a, b, LAST, preferred_element_type=F32)


def chip_shift(value, step):
    devices = lax.axis_size("mp")
    chips = devices // 2
    pairs = [
        (2 * z + c, 2 * ((z + step) % chips) + c) for z in range(chips) for c in range(2)
    ]
    return lax.ppermute(value, "mp", pairs)


def core_swap(value):
    return lax.ppermute(value, "mp", [(i, i ^ 1) for i in range(lax.axis_size("mp"))])


def ring_gather(own):
    reach = lax.axis_size("mp") // 4
    half = own.shape[0] // 2
    up = down = own
    chunks = [own]
    for _ in range(reach - 1):
        up, down = chip_shift(up, 1), chip_shift(down, -1)
        chunks += [up, down]
    chunks += [chip_shift(up[:half], 1), chip_shift(down[half:], -1)]
    return jnp.concatenate(chunks, axis=0)


def ring_scatter(parts, rows):
    reach = lax.axis_size("mp") // 4
    half = rows // 2

    def chunk(place):
        return parts[place * rows : (place + 1) * rows].astype(F32)

    far = chunk(2 * reach - 1)
    up = chip_shift(far[:half].astype(BF), 1).astype(F32)
    down = chip_shift(far[half:].astype(BF), -1).astype(F32)
    up_next, down_next = chunk(2 * reach - 2), chunk(2 * reach - 3)
    up = jnp.concatenate([up_next[:half] + up, up_next[half:]], axis=0)
    down = jnp.concatenate([down_next[:half], down_next[half:] + down], axis=0)
    for distance in range(reach - 1, 0, -1):
        up = chip_shift(up.astype(BF), 1).astype(F32)
        down = chip_shift(down.astype(BF), -1).astype(F32)
        if distance > 1:
            up = up + chunk(2 * distance - 2)
            down = down + chunk(2 * distance - 3)
    return (chunk(0) + up + down).astype(BF)


def per_device(hidden_in, out_grad, neighbours, counts, slot_owner, w_query, w_key, w_value, w_out):
    groups = lax.axis_size("dp")
    spans = counts.shape[0]
    slots_group = spans * MAXN
    src_slots = slot_owner.shape[0]
    capacity = src_slots // groups
    rows_dev = neighbours.shape[1]
    enc_width = neighbours.shape[2]
    heads_dev = w_query.shape[1] // DH
    query_width = w_query.shape[1]
    score_scale = 1.0 / math.sqrt(DH)
    tokens_dev = hidden_in.shape[0]
    span_len = tokens_dev // spans

    both = lax.all_gather(
        jnp.concatenate([hidden_in, out_grad], axis=0), "mp", axis=1, tiled=True
    )

    slot_order = jnp.arange(src_slots, dtype=jnp.int32)
    dest_group = jnp.where(slot_owner >= 0, slot_owner // slots_group, -1)
    earlier = (dest_group[None, :] == dest_group[:, None]) & (
        slot_order[None, :] < slot_order[:, None]
    )
    rank_in = jnp.sum(earlier.astype(jnp.int32), axis=1)
    position = jnp.where(slot_owner >= 0, dest_group * capacity + rank_in, -1)
    picked = position[None, :] == slot_order[:, None]
    source = jnp.sum(jnp.where(picked, slot_order[None, :], 0), axis=1)
    filled = jnp.any(picked, axis=1)
    tags = jnp.where(filled, jnp.take(slot_owner, source) % slots_group, -1)
    send_rows = jnp.concatenate(
        [
            jnp.take(neighbours, source, axis=0),
            jnp.broadcast_to(tags.astype(BF)[:, None, None], (src_slots, rows_dev, 128)),
        ],
        axis=2,
    )
    got = lax.all_to_all(
        send_rows.reshape(groups, capacity, rows_dev, enc_width + 128),
        "dp",
        split_axis=0,
        concat_axis=0,
        tiled=True,
    ).reshape(src_slots, rows_dev, enc_width + 128)
    local_slot = got[:, 0, enc_width].astype(jnp.int32)
    wanted = jnp.arange(slots_group, dtype=jnp.int32)
    matches = local_slot[None, :] == wanted[:, None]
    chosen = jnp.sum(jnp.where(matches, slot_order[None, :], 0), axis=1)
    safe_slot = jnp.maximum(local_slot, 0)
    own = jnp.take(got[:, :, :enc_width], chosen, axis=0)
    chunk_rows = MAXN * rows_dev
    own = own.reshape(spans, chunk_rows, enc_width)

    near = [ring_gather(own[c]) for c in range(spans)]
    far = [core_swap(x) for x in near]

    x_all, dy_all = both[:tokens_dev], both[tokens_dev:]
    queries = dot(x_all, w_query).astype(BF)
    grad_attended = dot_t(dy_all, w_out).astype(BF)
    heads = [slice(h * DH, (h + 1) * DH) for h in range(heads_dev)]
    query_enc = [dot_t(queries[:, s], w_key[:, s]).astype(BF) for s in heads]
    grad_enc = [dot_t(grad_attended[:, s], w_value[:, s]).astype(BF) for s in heads]

    half_keys = near[0].shape[0]
    key_slot = (jnp.arange(half_keys, dtype=jnp.int32) // rows_dev) % MAXN
    attended, grads = [], []
    for c in range(spans):
        tokens = slice(c * span_len, (c + 1) * span_len)
        rows = jnp.concatenate([e[tokens] for e in query_enc + grad_enc], axis=0)
        live = (key_slot < counts[c])[None, :]
        middle = heads_dev * span_len
        products = [dot_t(rows, near[c]), dot_t(rows, far[c])]
        scores = [jnp.where(live, p[:middle] * score_scale, -jnp.inf) for p in products]
        grad_weights = [p[middle:] for p in products]
        peak = jnp.maximum(
            jnp.max(scores[0], axis=-1, keepdims=True), jnp.max(scores[1], axis=-1, keepdims=True)
        )
        exponent = [jnp.exp(s - peak) for s in scores]
        total = sum(jnp.sum(e, axis=-1, keepdims=True) for e in exponent)
        weights = [e / total for e in exponent]
        inner = sum(
            jnp.sum(w * g, axis=-1, keepdims=True)
            for w, g in zip(weights, grad_weights, strict=True)
        )
        weights_bf = [w.astype(BF) for w in weights]
        grad_scores = [
            (w * (g - inner) * score_scale).astype(BF)
            for w, g in zip(weights, grad_weights, strict=True)
        ]
        mixed = (dot(weights_bf[0], near[c]) + dot(weights_bf[1], far[c])).astype(BF)
        attended.append(
            jnp.concatenate(
                [
                    dot(mixed[h * span_len : (h + 1) * span_len], w_value[:, s])
                    for h, s in enumerate(heads)
                ],
                axis=1,
            ).astype(BF)
        )
        columns = [
            jnp.concatenate([g, w], axis=0)
            for g, w in zip(grad_scores, weights_bf, strict=True)
        ]
        here, there = [
            lax.dot_general(b, rows, (((0,), (0,)), ((), ())), preferred_element_type=F32)
            for b in columns
        ]
        there = core_swap(there.astype(BF))
        grads.append(ring_scatter((here + there.astype(F32)).astype(BF), chunk_rows))

    out_part = dot(jnp.concatenate(attended, axis=0), w_out)
    layer_out = lax.psum_scatter(out_part.astype(BF), "mp", scatter_dimension=1, tiled=True)

    grad_rows = jnp.stack(grads).reshape(slots_group, rows_dev, enc_width)
    returned = lax.all_to_all(
        jnp.take(grad_rows, safe_slot, axis=0).reshape(groups, capacity, rows_dev, enc_width),
        "dp",
        split_axis=0,
        concat_axis=0,
        tiled=True,
    ).reshape(src_slots, rows_dev, enc_width)
    neighbour_grad = jnp.where(
        (slot_owner >= 0)[:, None, None],
        jnp.take(returned, jnp.maximum(position, 0), axis=0),
        jnp.zeros((), BF),
    )
    return (layer_out, neighbour_grad)


def solution(mesh):
    return jax.shard_map(
        per_device,
        mesh=mesh,
        in_specs=(
            P("dp", "mp"),
            P("dp", "mp"),
            P("dp", "mp", None),
            P("dp"),
            P("dp"),
            P(None, "mp"),
            P(None, "mp"),
            P(None, "mp"),
            P("mp", None),
        ),
        out_specs=(P("dp", "mp"), P("dp", "mp", None)),
        check_vma=False,
    )
```

```python
import math

import jax
import jax.numpy as jnp
from jax import lax
from jax.sharding import PartitionSpec as P

DH = 128
MAXN = 10
BF = jnp.bfloat16
F32 = jnp.float32
LAST = (((1,), (1,)), ((), ()))


def dot(a, b):
    return jnp.dot(a, b, preferred_element_type=F32)


def dot_t(a, b):
    return lax.dot_general(a, b, LAST, preferred_element_type=F32)


def chip_shift(value, step):
    devices = lax.axis_size("mp")
    chips = devices // 2
    pairs = [
        (2 * z + c, 2 * ((z + step) % chips) + c) for z in range(chips) for c in range(2)
    ]
    return lax.ppermute(value, "mp", pairs)


def core_swap(value):
    return lax.ppermute(value, "mp", [(i, i ^ 1) for i in range(lax.axis_size("mp"))])


def ring_gather(own):
    reach = lax.axis_size("mp") // 4
    half = own.shape[0] // 2
    up = down = own
    chunks = [own]
    for _ in range(reach - 1):
        up, down = chip_shift(up, 1), chip_shift(down, -1)
        chunks += [up, down]
    chunks.append(
        jnp.concatenate([chip_shift(up[:half], 1), chip_shift(down[half:], -1)], axis=0)
    )
    return chunks


def ring_scatter(chunks):
    reach = lax.axis_size("mp") // 4
    half = chunks[0].shape[0] // 2
    far, up_next, down_next = chunks[2 * reach - 1], chunks[2 * reach - 2], chunks[2 * reach - 3]
    up = chip_shift(far[:half].astype(BF), 1).astype(F32)
    down = chip_shift(far[half:].astype(BF), -1).astype(F32)
    up = jnp.concatenate([up_next[:half] + up, up_next[half:]], axis=0)
    down = jnp.concatenate([down_next[:half], down_next[half:] + down], axis=0)
    for distance in range(reach - 1, 0, -1):
        up = chip_shift(up.astype(BF), 1).astype(F32)
        down = chip_shift(down.astype(BF), -1).astype(F32)
        if distance > 1:
            up = up + chunks[2 * distance - 2]
            down = down + chunks[2 * distance - 3]
    return (chunks[0] + up + down).astype(BF)


def relative_blocks(array, axis):
    devices = lax.axis_size("mp")
    chips, reach = devices // 2, devices // 4
    me = lax.axis_index("mp")
    width = array.shape[axis] // devices
    order = [0]
    for distance in range(1, reach):
        order += [-distance, distance]
    order.append(reach)
    blocks = []
    for flip in range(2):
        for distance in order:
            device = (me // 2 + distance + chips) % chips * 2 + (me % 2 + flip) % 2
            blocks.append(lax.dynamic_slice_in_dim(array, device * width, width, axis))
    return jnp.concatenate(blocks, axis=axis)


def per_device(hidden_in, out_grad, neighbours, counts, slot_owner, w_query, w_key, w_value, w_out):
    groups = lax.axis_size("dp")
    spans = counts.shape[0]
    slots_group = spans * MAXN
    src_slots = slot_owner.shape[0]
    capacity = src_slots // groups
    rows_dev = neighbours.shape[1]
    enc_width = neighbours.shape[2]
    heads_dev = w_query.shape[1] // DH
    query_width = w_query.shape[1]
    score_scale = 1.0 / math.sqrt(DH)
    tokens_dev = hidden_in.shape[0]
    span_len = tokens_dev // spans
    core = lax.axis_index("mp") % 2

    def mine(array, span):
        return lax.dynamic_slice_in_dim(array, span * span_len, span_len, 0)

    x_ring = ring_gather(hidden_in)
    dy_ring = ring_gather(out_grad)

    slot_order = jnp.arange(src_slots, dtype=jnp.int32)
    dest_group = jnp.where(slot_owner >= 0, slot_owner // slots_group, -1)
    earlier = (dest_group[None, :] == dest_group[:, None]) & (
        slot_order[None, :] < slot_order[:, None]
    )
    rank_in = jnp.sum(earlier.astype(jnp.int32), axis=1)
    position = jnp.where(slot_owner >= 0, dest_group * capacity + rank_in, -1)
    picked = position[None, :] == slot_order[:, None]
    source = jnp.sum(jnp.where(picked, slot_order[None, :], 0), axis=1)
    filled = jnp.any(picked, axis=1)
    tags = jnp.where(filled, jnp.take(slot_owner, source) % slots_group, -1)
    send_rows = jnp.concatenate(
        [
            jnp.take(neighbours, source, axis=0),
            jnp.broadcast_to(tags.astype(BF)[:, None, None], (src_slots, rows_dev, 128)),
        ],
        axis=2,
    )
    got = lax.all_to_all(
        send_rows.reshape(groups, capacity, rows_dev, enc_width + 128),
        "dp",
        split_axis=0,
        concat_axis=0,
        tiled=True,
    ).reshape(src_slots, rows_dev, enc_width + 128)
    local_slot = got[:, 0, enc_width].astype(jnp.int32)
    wanted = jnp.arange(slots_group, dtype=jnp.int32)
    matches = local_slot[None, :] == wanted[:, None]
    chosen = jnp.sum(jnp.where(matches, slot_order[None, :], 0), axis=1)
    safe_slot = jnp.maximum(local_slot, 0)
    chunk_rows = MAXN * rows_dev

    def rows_of(span):
        slots = lax.dynamic_slice_in_dim(chosen, span * MAXN, MAXN)
        return jnp.take(got[:, :, :enc_width], slots, axis=0).reshape(chunk_rows, enc_width)

    given = core_swap(rows_of(1 - core))
    kept = ring_gather(rows_of(core))
    taken = ring_gather(given)
    rows = jnp.concatenate(kept + taken, axis=0)

    w_key_both = [w_key, core_swap(w_key)]
    w_value_both = [w_value, core_swap(w_value)]
    w_query_rel = relative_blocks(w_query, 0)
    w_out_rel = relative_blocks(w_out, 1)

    x_near = jnp.concatenate(x_ring, axis=1)
    dy_near = jnp.concatenate(dy_ring, axis=1)
    x_all = jnp.concatenate([x_near, core_swap(x_near)], axis=1)
    dy_all = jnp.concatenate([dy_near, core_swap(dy_near)], axis=1)
    queries = dot(x_all, w_query_rel).astype(BF)
    grad_attended = dot_t(dy_all, w_out_rel).astype(BF)
    pair = jnp.concatenate([queries, grad_attended], axis=1)
    pair = [mine(pair, core), core_swap(mine(pair, 1 - core))]

    heads = [slice(h * DH, (h + 1) * DH) for h in range(heads_dev)]
    query_enc, grad_enc = [], []
    for p, wk, wv in zip(pair, w_key_both, w_value_both, strict=True):
        query_enc += [dot_t(p[:, :query_width][:, s], wk[:, s]).astype(BF) for s in heads]
        grad_enc += [dot_t(p[:, query_width:][:, s], wv[:, s]).astype(BF) for s in heads]
    lines = jnp.concatenate(query_enc + grad_enc, axis=0)
    middle = lines.shape[0] // 2

    key_slot = (jnp.arange(rows.shape[0], dtype=jnp.int32) // rows_dev) % MAXN
    live = (key_slot < lax.dynamic_index_in_dim(counts, core, keepdims=False))[None, :]
    products = dot_t(lines, rows)
    scores = jnp.where(live, products[:middle] * score_scale, -jnp.inf)
    grad_weights = products[middle:]
    peak = jnp.max(scores, axis=-1, keepdims=True)
    exponent = jnp.exp(scores - peak)
    weights = exponent / jnp.sum(exponent, axis=-1, keepdims=True)
    inner = jnp.sum(weights * grad_weights, axis=-1, keepdims=True)
    weights_bf = weights.astype(BF)
    grad_scores = (weights * (grad_weights - inner) * score_scale).astype(BF)
    columns = jnp.concatenate([grad_scores, weights_bf], axis=0)
    grads = lax.dot_general(columns, lines, (((0,), (0,)), ((), ())), preferred_element_type=F32)
    chips = rows.shape[0] // (2 * chunk_rows)

    def chunks_of(array, first):
        return [array[(first + i) * chunk_rows : (first + i + 1) * chunk_rows] for i in range(chips)]

    grad_kept = ring_scatter(chunks_of(grads, 0))
    grad_given = core_swap(ring_scatter(chunks_of(grads, chips)))
    grad_rows = jnp.where(
        core == 0,
        jnp.concatenate([grad_kept, grad_given], axis=0),
        jnp.concatenate([grad_given, grad_kept], axis=0),
    ).reshape(slots_group, rows_dev, enc_width)

    mixed = dot(weights_bf, rows).astype(BF)
    attended = [
        jnp.concatenate(
            [
                dot(mixed[(i * heads_dev + h) * span_len :][:span_len], wv[:, s])
                for h, s in enumerate(heads)
            ],
            axis=1,
        ).astype(BF)
        for i, wv in enumerate(w_value_both)
    ]
    attended[1] = core_swap(attended[1])
    attended = jnp.where(
        core == 0,
        jnp.concatenate(attended, axis=0),
        jnp.concatenate(attended[::-1], axis=0),
    )
    out_part = dot(attended, w_out_rel)
    out_half = out_part.shape[1] // 2
    out_pair = out_part[:, :out_half] + core_swap(out_part[:, out_half:].astype(BF)).astype(F32)
    width = out_half // chips
    layer_out = ring_scatter([out_pair[:, i * width : (i + 1) * width] for i in range(chips)])

    returned = lax.all_to_all(
        jnp.take(grad_rows, safe_slot, axis=0).reshape(groups, capacity, rows_dev, enc_width),
        "dp",
        split_axis=0,
        concat_axis=0,
        tiled=True,
    ).reshape(src_slots, rows_dev, enc_width)
    neighbour_grad = jnp.where(
        (slot_owner >= 0)[:, None, None],
        jnp.take(returned, jnp.maximum(position, 0), axis=0),
        jnp.zeros((), BF),
    )
    return (layer_out, neighbour_grad)


def solution(mesh):
    return jax.shard_map(
        per_device,
        mesh=mesh,
        in_specs=(
            P("dp", "mp"),
            P("dp", "mp"),
            P("dp", "mp", None),
            P("dp"),
            P("dp"),
            P(None, "mp"),
            P(None, "mp"),
            P(None, "mp"),
            P("mp", None),
        ),
        out_specs=(P("dp", "mp"), P("dp", "mp", None)),
        check_vma=False,
    )
```

```python
import functools
import math

import jax
import jax.numpy as jnp
from jax import lax
from jax.experimental import pallas as pl
from jax.experimental.pallas import tpu as pltpu
from jax.sharding import PartitionSpec as P

DH = 128
MAXN = 10
BF = jnp.bfloat16
F32 = jnp.float32
LAST = (((1,), (1,)), ((), ()))
FIRST = (((0,), (0,)), ((), ()))
CHIP_ORDER = (0, -1, 1, -2, 2, -3, 3, 4)
PAIRS = 4


def dot(a, b):
    return jnp.dot(a, b, preferred_element_type=F32)


def dot_t(a, b):
    return lax.dot_general(a, b, LAST, preferred_element_type=F32)


def chip_shift(value, step):
    devices = lax.axis_size("mp")
    chips = devices // 2
    pairs = [
        (2 * z + c, 2 * ((z + step) % chips) + c) for z in range(chips) for c in range(2)
    ]
    return lax.ppermute(value, "mp", pairs)


def core_swap(value):
    return lax.ppermute(value, "mp", [(i, i ^ 1) for i in range(lax.axis_size("mp"))])


def chip_swap(value):
    return lax.ppermute(value, "mp", [(i, i ^ 2) for i in range(lax.axis_size("mp"))])


def plane_shift(value, phase, step):
    groups, devices = lax.axis_size("dp"), lax.axis_size("mp")
    side = math.isqrt(groups)
    pairs = []
    for g in range(groups):
        x, y = g // side, g % side
        for m in range(devices):
            along_y = m % 2 == phase
            to = x * side + (y + step) % side if along_y else (x + step) % side * side + y
            pairs.append((g * devices + m, to * devices + m))
    return lax.ppermute(value, ("dp", "mp"), pairs)


def plane_gather(piece, phase, place):
    rows = piece.shape[0]
    side = math.isqrt(lax.axis_size("dp"))
    half = rows // 2
    up, down = plane_shift(piece, phase, 1), plane_shift(piece, phase, -1)
    far = [plane_shift(up[:half], phase, 1), plane_shift(down[half:], phase, -1)]
    whole = jnp.zeros((side * rows, piece.shape[1]), piece.dtype)
    for value, offset in (
        (piece, 0), (up, side - 1), (down, 1), (far[0], 2), (far[1], 2)
    ):
        start = (place + offset) % side * rows + (half if value is far[1] else 0)
        whole = lax.dynamic_update_slice_in_dim(whole, value, start, 0)
    return whole


def ring_gather(own):
    reach = lax.axis_size("mp") // 4
    half = own.shape[0] // 2
    up = down = own
    chunks = [own]
    for _ in range(reach - 1):
        up, down = chip_shift(up, 1), chip_shift(down, -1)
        chunks += [up, down]
    chunks.append(
        jnp.concatenate([chip_shift(up[:half], 1), chip_shift(down[half:], -1)], axis=0)
    )
    return chunks


def ring_scatter(chunks):
    reach = lax.axis_size("mp") // 4
    half = chunks[0].shape[0] // 2
    far, up_next, down_next = chunks[2 * reach - 1], chunks[2 * reach - 2], chunks[2 * reach - 3]
    up = chip_shift(far[:half].astype(BF), 1).astype(F32)
    down = chip_shift(far[half:].astype(BF), -1).astype(F32)
    up = jnp.concatenate([up_next[:half] + up, up_next[half:]], axis=0)
    down = jnp.concatenate([down_next[:half], down_next[half:] + down], axis=0)
    for distance in range(reach - 1, 0, -1):
        up = chip_shift(up.astype(BF), 1).astype(F32)
        down = chip_shift(down.astype(BF), -1).astype(F32)
        if distance > 1:
            up = up + chunks[2 * distance - 2]
            down = down + chunks[2 * distance - 3]
    return (chunks[0] + up + down).astype(BF)


def project_kernel(place, near, far, w_query, w_out, queries, grads, q_sum, g_sum):
    step = pl.program_id(0)

    @pl.when(step == 0)
    def _():
        q_sum[...] = jnp.zeros_like(q_sum)
        g_sum[...] = jnp.zeros_like(g_sum)

    tokens = near.shape[1] // 2
    width = near.shape[2]
    first = place[pl.num_programs(0)] == 0
    parts = [jnp.where(first, near[0], far[0]), jnp.where(first, far[0], near[0])]
    for i, part in enumerate(parts):
        q_sum[...] += dot(part[:tokens], w_query[i * width : (i + 1) * width, :])
        g_sum[...] += dot_t(part[tokens:], w_out[:, i * width : (i + 1) * width])

    @pl.when(step == pl.num_programs(0) - 1)
    def _():
        queries[...] = q_sum[...].astype(BF)
        grads[...] = g_sum[...].astype(BF)


def project(place, near, far, w_query, w_out):
    chips, rows, width = near.shape
    features = w_query.shape[1]
    out = jax.ShapeDtypeStruct((rows // 2, features), BF)
    return pl.pallas_call(
        project_kernel,
        out_shape=(out, out),
        grid_spec=pltpu.PrefetchScalarGridSpec(
            num_scalar_prefetch=1,
            grid=(chips,),
            in_specs=[
                pl.BlockSpec((1, rows, width), lambda i, p: (i, 0, 0)),
                pl.BlockSpec((1, rows, width), lambda i, p: (i, 0, 0)),
                pl.BlockSpec((2 * width, features), lambda i, p: (p[i], 0)),
                pl.BlockSpec((features, 2 * width), lambda i, p: (0, p[i])),
            ],
            out_specs=[
                pl.BlockSpec((rows // 2, features), lambda i, p: (0, 0)),
                pl.BlockSpec((rows // 2, features), lambda i, p: (0, 0)),
            ],
            scratch_shapes=[
                pltpu.VMEM((rows // 2, features), F32),
                pltpu.VMEM((rows // 2, features), F32),
            ],
        ),
        compiler_params=pltpu.CompilerParams(vmem_limit_bytes=32 * 2**20),
        cost_estimate=pl.CostEstimate(
            flops=4 * rows * chips * width * features,
            bytes_accessed=8 * chips * width * (features + rows),
            transcendentals=0,
        ),
    )(place, near, far, w_query, w_out)


def out_kernel(place, attended, w_out, mine, other):
    width = w_out.shape[1] // 2
    parts = [dot(attended[...], w_out[:, i * width : (i + 1) * width]) for i in range(2)]
    first = place[pl.num_programs(0)] == 0
    mine[0] = jnp.where(first, parts[0], parts[1])
    other[0] = jnp.where(first, parts[1], parts[0])


def project_out(place, attended, w_out):
    chips = place.shape[0] - 1
    tokens, features = attended.shape
    width = w_out.shape[1] // (2 * chips)
    out = jax.ShapeDtypeStruct((chips, tokens, width), F32)
    return pl.pallas_call(
        out_kernel,
        out_shape=(out, out),
        grid_spec=pltpu.PrefetchScalarGridSpec(
            num_scalar_prefetch=1,
            grid=(chips,),
            in_specs=[
                pl.BlockSpec((tokens, features), lambda i, p: (0, 0)),
                pl.BlockSpec((features, 2 * width), lambda i, p: (0, p[i])),
            ],
            out_specs=[
                pl.BlockSpec((1, tokens, width), lambda i, p: (i, 0, 0)),
                pl.BlockSpec((1, tokens, width), lambda i, p: (i, 0, 0)),
            ],
        ),
        compiler_params=pltpu.CompilerParams(vmem_limit_bytes=32 * 2**20),
        cost_estimate=pl.CostEstimate(
            flops=4 * tokens * features * width * chips,
            bytes_accessed=4 * chips * width * (features + 4 * tokens),
            transcendentals=0,
        ),
    )(place, attended, w_out)


def lines_kernel(queries, grads, w_key, w_value, lines):
    spans, _, _, length, _ = lines.shape
    for kind, (rows, weight) in enumerate(((queries, w_key), (grads, w_value))):
        made = dot_t(rows[0], weight[...]).astype(BF)
        for c in range(spans):
            lines[c, kind, 0] = made[c * length : (c + 1) * length]


def make_lines(pairs, weights, spans):
    blocks, tokens, width = pairs.shape
    heads = width // (2 * DH)
    enc = weights.shape[0]
    length = tokens // spans

    def part(kind):
        return lambda i: (i // heads, 0, kind * heads + i % heads)

    def column(kind):
        return lambda i: (0, i // heads * 2 * heads + kind * heads + i % heads)

    return pl.pallas_call(
        lines_kernel,
        out_shape=jax.ShapeDtypeStruct((spans, 2, blocks * heads, length, enc), BF),
        grid=(blocks * heads,),
        in_specs=[
            pl.BlockSpec((1, tokens, DH), part(0)),
            pl.BlockSpec((1, tokens, DH), part(1)),
            pl.BlockSpec((enc, DH), column(0)),
            pl.BlockSpec((enc, DH), column(1)),
        ],
        out_specs=pl.BlockSpec((spans, 2, 1, length, enc), lambda i: (0, 0, i, 0, 0)),
        compiler_params=pltpu.CompilerParams(vmem_limit_bytes=32 * 2**20),
        cost_estimate=pl.CostEstimate(
            flops=2 * tokens * width * blocks * enc,
            bytes_accessed=2 * enc * (width * blocks + 2 * tokens * blocks * heads),
            transcendentals=0,
        ),
    )(pairs, pairs, weights, weights)


def attended_kernel(mixed, w_value, out):
    spans, _, length, enc = mixed.shape
    rows = jnp.concatenate([mixed[c, 0] for c in range(spans)], axis=0)
    out[0] = dot(rows, w_value[...])


def make_attended(mixed, weights, heads):
    spans, count, length, enc = mixed.shape
    return pl.pallas_call(
        attended_kernel,
        out_shape=jax.ShapeDtypeStruct((count, spans * length, DH), F32),
        grid=(count,),
        in_specs=[
            pl.BlockSpec((spans, 1, length, enc), lambda i: (0, i, 0, 0)),
            pl.BlockSpec((enc, DH), lambda i: (0, i // heads * 2 * heads + heads + i % heads)),
        ],
        out_specs=pl.BlockSpec((1, spans * length, DH), lambda i: (i, 0, 0)),
        compiler_params=pltpu.CompilerParams(vmem_limit_bytes=32 * 2**20),
        cost_estimate=pl.CostEstimate(
            flops=2 * spans * length * enc * DH * count,
            bytes_accessed=2 * enc * count * (DH + spans * length),
            transcendentals=0,
        ),
    )(mixed, weights)


def per_device(hidden_in, out_grad, neighbours, counts, slot_owner, w_query, w_key, w_value, w_out):
    groups = lax.axis_size("dp")
    spans = counts.shape[0]
    slots_group = spans * MAXN
    src_slots = slot_owner.shape[0]
    capacity = src_slots // groups
    rows_dev = neighbours.shape[1]
    enc_width = neighbours.shape[2]
    heads_dev = w_query.shape[1] // DH
    score_scale = 1.0 / math.sqrt(DH)
    tokens_dev = hidden_in.shape[0]
    span_len = tokens_dev // spans
    chips = lax.axis_size("mp") // 2
    chip, core = lax.axis_index("mp") // 2, lax.axis_index("mp") % 2
    side = math.isqrt(groups)
    along_x, along_y = lax.axis_index("dp") // side, lax.axis_index("dp") % side
    inner_place = jnp.where(core == 0, along_y, along_x)
    outer_place = jnp.where(core == 0, along_x, along_y)
    place = jnp.stack([(chip + d + chips) % chips for d in CHIP_ORDER] + [core]).astype(jnp.int32)

    ring = ring_gather(jnp.concatenate([hidden_in, out_grad], axis=0))

    piece_rows = enc_width // groups
    start = (outer_place * side + inner_place) * piece_rows
    piece = jnp.concatenate(
        [lax.dynamic_slice_in_dim(w, start, piece_rows, 0) for w in (w_key, w_value)], axis=1
    )
    piece = jnp.concatenate([piece] + [chip_shift(piece, d) for d in (2, -2, 4)], axis=1)
    weights = plane_gather(plane_gather(piece, 0, inner_place), 1, outer_place)

    slot_order = jnp.arange(src_slots, dtype=jnp.int32)
    dest_group = jnp.where(slot_owner >= 0, slot_owner // slots_group, -1)
    earlier = (dest_group[None, :] == dest_group[:, None]) & (
        slot_order[None, :] < slot_order[:, None]
    )
    rank_in = jnp.sum(earlier.astype(jnp.int32), axis=1)
    position = jnp.where(slot_owner >= 0, dest_group * capacity + rank_in, -1)
    picked = position[None, :] == slot_order[:, None]
    source = jnp.sum(jnp.where(picked, slot_order[None, :], 0), axis=1)
    filled = jnp.any(picked, axis=1)
    tags = jnp.where(filled, jnp.take(slot_owner, source) % slots_group, -1)
    send_rows = jnp.concatenate(
        [
            jnp.take(neighbours, source, axis=0),
            jnp.broadcast_to(tags.astype(BF)[:, None, None], (src_slots, rows_dev, 128)),
        ],
        axis=2,
    )
    got = lax.all_to_all(
        send_rows.reshape(groups, capacity, rows_dev, enc_width + 128),
        "dp",
        split_axis=0,
        concat_axis=0,
        tiled=True,
    ).reshape(src_slots, rows_dev, enc_width + 128)
    local_slot = got[:, 0, enc_width].astype(jnp.int32)
    wanted = jnp.arange(slots_group, dtype=jnp.int32)
    matches = local_slot[None, :] == wanted[:, None]
    chosen = jnp.sum(jnp.where(matches, slot_order[None, :], 0), axis=1)
    safe_slot = jnp.maximum(local_slot, 0)
    chunk_rows = MAXN * rows_dev
    own = jnp.take(got[:, :, :enc_width], chosen, axis=0)
    own = own.reshape(slots_group * rows_dev, enc_width)
    chip_rows = jnp.concatenate([own, chip_swap(own)], axis=0)
    chunks = jnp.concatenate([chip_rows, core_swap(chip_rows)], axis=0)
    chunks = chunks.reshape(4, spans, chunk_rows, enc_width)
    keys = [chunks[:, c].reshape(4 * chunk_rows, enc_width) for c in range(spans)]

    near = jnp.stack(ring)
    queries, grad_attended = project(place, near, core_swap(near), w_query, w_out)
    pair = jnp.concatenate([queries, grad_attended], axis=1)
    pairs = jnp.stack([pair] + [chip_shift(pair, d) for d in (2, -2, 4)])
    lines = make_lines(pairs, weights, spans)
    heads = lines.shape[2]
    middle = heads * span_len
    lines = lines.reshape(spans, 2 * middle, enc_width)

    key_slot = (jnp.arange(4 * chunk_rows, dtype=jnp.int32) // rows_dev) % MAXN
    exponents, grad_weights, stats, mixed = [], [], [], []
    for c in range(spans):
        products = dot_t(lines[c], keys[c])
        live = (key_slot < counts[c])[None, :]
        scores = jnp.where(live, products[:middle] * score_scale, -jnp.inf)
        peak = jnp.max(scores, axis=-1)
        exponent = jnp.exp(scores - peak[:, None])
        grad_weight = products[middle:]
        stats.append(
            jnp.stack([peak, jnp.sum(exponent, -1), jnp.sum(exponent * grad_weight, -1)])
        )
        exponents.append(exponent)
        grad_weights.append(grad_weight)
        mixed.append(dot(exponent.astype(BF), keys[c]).astype(BF).reshape(heads, span_len, -1))
    partial = make_attended(jnp.stack(mixed), weights, heads_dev)
    partial = partial.reshape(PAIRS, heads_dev * tokens_dev, DH)
    stats = jnp.stack(stats, axis=1).reshape(3, spans, PAIRS, heads_dev * span_len)
    others = []
    for shift, to, order in ((2, 2, (2, 0, 3, 1)), (-2, 1, (1, 3, 0, 2)), (4, 3, (3, 2, 1, 0))):
        message = jnp.stack([stats[:, :, i] for i in order], axis=2).reshape(-1, DH)
        message = chip_shift(jnp.concatenate([partial[to], message], axis=0), shift)
        others.append(
            (message[: partial.shape[1]], message[partial.shape[1] :].reshape(stats.shape))
        )
    attended_parts = [partial[0]] + [a for a, _ in others]
    all_stats = jnp.stack([stats] + [s for _, s in others])
    top = jnp.max(all_stats[:, 0], axis=0)
    factors = jnp.exp(all_stats[:, 0] - top)
    total = jnp.sum(factors * all_stats[:, 1], axis=0)
    inner = jnp.sum(factors * all_stats[:, 2], axis=0) / total
    factors = factors / total

    def tokens_first(array):
        spread = array[:, 0].reshape(spans, heads_dev, span_len)
        return jnp.transpose(spread, (1, 0, 2)).reshape(heads_dev * tokens_dev, 1)

    attended = sum(
        part * tokens_first(f) for part, f in zip(attended_parts, factors, strict=True)
    ).astype(BF)
    attended = jnp.concatenate(
        [attended[h * tokens_dev : (h + 1) * tokens_dev] for h in range(heads_dev)], axis=1
    )

    grads = []
    for c in range(spans):
        weight = exponents[c] * factors[0, c].reshape(middle, 1)
        grad_score = weight * (grad_weights[c] - inner[c].reshape(middle, 1)) * score_scale
        columns = jnp.concatenate([grad_score.astype(BF), weight.astype(BF)], axis=0)
        grads.append(
            lax.dot_general(columns, lines[c], FIRST, preferred_element_type=F32).reshape(
                4, chunk_rows, enc_width
            )
        )
    grads = jnp.stack(grads, axis=1)
    summed = grads[:2] + core_swap(grads[2:].astype(BF)).astype(F32)
    grad_rows = (summed[0] + chip_swap(summed[1].astype(BF)).astype(F32)).astype(BF)
    grad_rows = grad_rows.reshape(slots_group, rows_dev, enc_width)

    out_mine, out_other = project_out(place, attended, w_out)
    out_pair = out_mine + core_swap(out_other)
    layer_out = ring_scatter([out_pair[i] for i in range(chips)])

    returned = lax.all_to_all(
        jnp.take(grad_rows, safe_slot, axis=0).reshape(groups, capacity, rows_dev, enc_width),
        "dp",
        split_axis=0,
        concat_axis=0,
        tiled=True,
    ).reshape(src_slots, rows_dev, enc_width)
    neighbour_grad = jnp.where(
        (slot_owner >= 0)[:, None, None],
        jnp.take(returned, jnp.maximum(position, 0), axis=0),
        jnp.zeros((), BF),
    )
    return (layer_out, neighbour_grad)


def solution(mesh):
    return jax.shard_map(
        per_device,
        mesh=mesh,
        in_specs=(
            P("dp", "mp"),
            P("dp", "mp"),
            P("dp", "mp", None),
            P("dp"),
            P("dp"),
            P(None, "mp"),
            P(None, "mp"),
            P(None, "mp"),
            P("mp", None),
        ),
        out_specs=(P("dp", "mp"), P("dp", "mp", None)),
        check_vma=False,
    )
```

```python
import functools
import math

import jax
import jax.numpy as jnp
from jax import lax
from jax.experimental import pallas as pl
from jax.experimental.pallas import tpu as pltpu
from jax.sharding import PartitionSpec as P

DH = 128
MAXN = 10
BF = jnp.bfloat16
F32 = jnp.float32
LAST = (((1,), (1,)), ((), ()))
FIRST = (((0,), (0,)), ((), ()))


def dot(a, b):
    return jnp.dot(a, b, preferred_element_type=F32)


def dot_t(a, b):
    return lax.dot_general(a, b, LAST, preferred_element_type=F32)


def chip_shift(value, step):
    devices = lax.axis_size("mp")
    chips = devices // 2
    pairs = [
        (2 * z + c, 2 * ((z + step) % chips) + c) for z in range(chips) for c in range(2)
    ]
    return lax.ppermute(value, "mp", pairs)


def core_swap(value):
    return lax.ppermute(value, "mp", [(i, i ^ 1) for i in range(lax.axis_size("mp"))])


def tie(first, second):
    return lax.optimization_barrier((first, second))


def ring_step(ups, downs):
    return [chip_shift(u, 1) for u in ups], [chip_shift(d, -1) for d in downs]


def to_bf16(values):
    return [v.astype(BF) for v in values]


VMEM_LIMIT = 40 * 2**20


def in_vmem(count):
    return [pl.BlockSpec(memory_space=pltpu.VMEM)] * count


def out_kernel(core, attended, w_out, mine, other):
    width = w_out.shape[1] // 2
    parts = [dot(attended[...], w_out[:, i * width : (i + 1) * width]) for i in range(2)]
    first = core[0] == 0
    mine[0] = jnp.where(first, parts[0], parts[1])
    other[0] = jnp.where(first, parts[1], parts[0])


def project_out(core, attended, w_out, chips):
    tokens, features = attended.shape
    width = w_out.shape[1] // (2 * chips)
    out = jax.ShapeDtypeStruct((chips, tokens, width), F32)
    return pl.pallas_call(
        out_kernel,
        out_shape=(out, out),
        grid_spec=pltpu.PrefetchScalarGridSpec(
            num_scalar_prefetch=1,
            grid=(chips,),
            in_specs=[
                pl.BlockSpec((tokens, features), lambda i, p: (0, 0)),
                pl.BlockSpec((features, 2 * width), lambda i, p: (0, i)),
            ],
            out_specs=[
                pl.BlockSpec((1, tokens, width), lambda i, p: (i, 0, 0)),
                pl.BlockSpec((1, tokens, width), lambda i, p: (i, 0, 0)),
            ],
        ),
        compiler_params=pltpu.CompilerParams(vmem_limit_bytes=VMEM_LIMIT),
        cost_estimate=pl.CostEstimate(
            flops=4 * tokens * features * width * chips,
            bytes_accessed=4 * chips * width * (features + 4 * tokens),
            transcendentals=0,
        ),
    )(core, attended, w_out)


def lines_kernel(own, partner, key_own, value_own, key_partner, value_partner, lines):
    length, width = own.shape
    heads = width // (2 * DH)
    for kind, weights in enumerate(((key_own, key_partner), (value_own, value_partner))):
        for i, (pair, weight) in enumerate(zip((own, partner), weights)):
            for h in range(heads):
                part = slice((kind * heads + h) * DH, (kind * heads + h + 1) * DH)
                first = ((kind * 2 + i) * heads + h) * length
                made = dot_t(pair[:, part], weight[:, h * DH : (h + 1) * DH])
                lines[first : first + length] = made.astype(BF)


def make_lines(own, partner, weights):
    length, width = own.shape
    enc = weights[0].shape[0]
    rows = 2 * length * width // DH
    return pl.pallas_call(
        lines_kernel,
        out_shape=jax.ShapeDtypeStruct((rows, enc), BF),
        in_specs=in_vmem(6),
        out_specs=in_vmem(1)[0],
        compiler_params=pltpu.CompilerParams(vmem_limit_bytes=VMEM_LIMIT),
        cost_estimate=pl.CostEstimate(
            flops=2 * rows * DH * enc, bytes_accessed=4 * rows * enc, transcendentals=0
        ),
    )(own, partner, *weights)


def products_kernel(lines, *refs):
    keys = jnp.concatenate([r[...] for r in refs[:-1]], axis=0)
    refs[-1][...] = dot_t(lines[...], keys)


def make_products(lines, chunks):
    rows, enc = lines.shape
    count = sum(c.shape[0] for c in chunks)
    return pl.pallas_call(
        products_kernel,
        out_shape=jax.ShapeDtypeStruct((rows, count), F32),
        in_specs=in_vmem(1 + len(chunks)),
        out_specs=in_vmem(1)[0],
        compiler_params=pltpu.CompilerParams(vmem_limit_bytes=VMEM_LIMIT),
        cost_estimate=pl.CostEstimate(
            flops=2 * rows * count * enc,
            bytes_accessed=2 * enc * (rows + count) + 4 * rows * count,
            transcendentals=0,
        ),
    )(lines, *chunks)


def softmax_kernel(scale, per_slot, period, late, count, lines, early, *refs):
    keys = jnp.concatenate([r[...] for r in refs[:late]], axis=0)
    weights_out, grads_out = refs[late : late + 2], refs[late + 2 :]
    products = [early[...], dot_t(lines[...], keys)]
    middle = lines.shape[0] // 2
    scores = []
    for product in products:
        columns = lax.broadcasted_iota(jnp.int32, (middle, product.shape[1]), 1)
        live = (columns % period) // per_slot < count[0]
        scores.append(jnp.where(live, product[:middle] * scale, -jnp.inf))
    peak = functools.reduce(
        jnp.maximum, [jnp.max(part, axis=-1, keepdims=True) for part in scores]
    )
    exponents = [jnp.exp(part - peak) for part in scores]
    total = sum(jnp.sum(part, axis=-1, keepdims=True) for part in exponents)
    weights = [part / total for part in exponents]
    inner = sum(
        jnp.sum(w * p[middle:], axis=-1, keepdims=True) for w, p in zip(weights, products)
    )
    place = 0
    for weight, product, out in zip(weights, products, weights_out):
        score = weight * (product[middle:] - inner) * scale
        rounded = weight.astype(BF)
        out[...] = rounded
        columns = jnp.concatenate([score.astype(BF), rounded], axis=0)
        made = lax.dot_general(columns, lines[...], FIRST, preferred_element_type=F32)
        first = 0
        while first < made.shape[0]:
            out = grads_out[place]
            out[...] = made[first : first + out.shape[0]].astype(out.dtype)
            first += out.shape[0]
            place += 1


def make_softmax(count, lines, early, chunks, per_slot, shapes, scale):
    rows, enc = lines.shape
    late = sum(c.shape[0] for c in chunks)
    keys = early.shape[1] + late
    period = shapes[0][0]
    return pl.pallas_call(
        functools.partial(softmax_kernel, scale, per_slot, period, len(chunks)),
        out_shape=[
            jax.ShapeDtypeStruct((rows // 2, early.shape[1]), BF),
            jax.ShapeDtypeStruct((rows // 2, late), BF),
        ]
        + [jax.ShapeDtypeStruct((n, enc), kind) for n, kind in shapes],
        in_specs=[pl.BlockSpec(memory_space=pltpu.SMEM)] + in_vmem(2 + len(chunks)),
        out_specs=in_vmem(2 + len(shapes)),
        compiler_params=pltpu.CompilerParams(vmem_limit_bytes=VMEM_LIMIT),
        cost_estimate=pl.CostEstimate(
            flops=2 * rows * (late + keys) * enc,
            bytes_accessed=2 * enc * (rows + late + 2 * keys) + 4 * rows * keys,
            transcendentals=rows * keys // 2,
        ),
    )(count, lines, early, *chunks)


def attended_kernel(early_count, first, second, value_own, value_partner, *refs):
    own, partner = refs[-2:]
    chunks = [r[...] for r in refs[:-2]]
    mixed = dot(first[...], jnp.concatenate(chunks[:early_count], axis=0))
    mixed += dot(second[...], jnp.concatenate(chunks[early_count:], axis=0))
    mixed = mixed.astype(BF)
    length, width = own.shape
    for i, (weight, out) in enumerate(((value_own, own), (value_partner, partner))):
        for h in range(width // DH):
            rows = slice((i * (width // DH) + h) * length, (i * (width // DH) + h + 1) * length)
            part = slice(h * DH, (h + 1) * DH)
            out[:, part] = dot(mixed[rows], weight[:, part]).astype(BF)


def make_attended(weights, values, early, late, length):
    rows, enc = weights[0].shape[0], values[0].shape[0]
    keys = weights[0].shape[1] + weights[1].shape[1]
    out = jax.ShapeDtypeStruct((length, values[0].shape[1]), BF)
    return pl.pallas_call(
        functools.partial(attended_kernel, len(early)),
        out_shape=(out, out),
        in_specs=in_vmem(4 + len(early) + len(late)),
        out_specs=in_vmem(2),
        compiler_params=pltpu.CompilerParams(vmem_limit_bytes=VMEM_LIMIT),
        cost_estimate=pl.CostEstimate(
            flops=2 * rows * keys * enc, bytes_accessed=2 * keys * (rows + enc), transcendentals=0
        ),
    )(*weights, *values, *early, *late)


def project_kernel(both, w_query, w_out, pair, q_sum, g_sum):
    step = pl.program_id(0)
    tokens, features = q_sum.shape

    @pl.when(step == 0)
    def _():
        q_sum[...] = jnp.zeros_like(q_sum)
        g_sum[...] = jnp.zeros_like(g_sum)

    q_sum[...] += dot(both[:tokens], w_query[...])
    g_sum[...] += dot_t(both[tokens:], w_out[...])

    @pl.when(step == pl.num_programs(0) - 1)
    def _():
        pair[:, :features] = q_sum[...].astype(BF)
        pair[:, features:] = g_sum[...].astype(BF)


def project(both, w_query, w_out):
    rows, model = both.shape
    features = w_query.shape[1]
    steps = 8
    width = model // steps
    return pl.pallas_call(
        project_kernel,
        out_shape=jax.ShapeDtypeStruct((rows // 2, 2 * features), BF),
        grid=(steps,),
        in_specs=[
            pl.BlockSpec((rows, width), lambda i: (0, i)),
            pl.BlockSpec((width, features), lambda i: (i, 0)),
            pl.BlockSpec((features, width), lambda i: (0, i)),
        ],
        out_specs=pl.BlockSpec((rows // 2, 2 * features), lambda i: (0, 0)),
        scratch_shapes=[
            pltpu.VMEM((rows // 2, features), F32),
            pltpu.VMEM((rows // 2, features), F32),
        ],
        compiler_params=pltpu.CompilerParams(vmem_limit_bytes=32 * 2**20),
        cost_estimate=pl.CostEstimate(
            flops=2 * rows * model * features,
            bytes_accessed=2 * model * (2 * features + rows),
            transcendentals=0,
        ),
    )(both, w_query, w_out)


def pick_kernel(parts, source, rows, *outs):
    count, _, width = outs[0].shape
    for i in range(count * parts):
        value = rows[jnp.maximum(source[i], 0), :, :width]
        outs[i // count][i % count] = jnp.where(source[i] >= 0, value, jnp.zeros_like(value))


def pick(rows, source, width=None, parts=1):
    shape = (source.shape[0] // parts, rows.shape[1], width or rows.shape[2])
    return pl.pallas_call(
        functools.partial(pick_kernel, parts),
        out_shape=[jax.ShapeDtypeStruct(shape, BF)] * parts,
        in_specs=[pl.BlockSpec(memory_space=pltpu.SMEM)] + in_vmem(1),
        out_specs=in_vmem(parts),
        cost_estimate=pl.CostEstimate(
            flops=0, bytes_accessed=4 * parts * math.prod(shape), transcendentals=0
        ),
    )(source.astype(jnp.int32), rows)


def pack_kernel(slots_group, owner, rows, hidden, grad, out, position, both, counts):
    both[: hidden.shape[0]] = hidden[...]
    both[hidden.shape[0] :] = grad[...]
    count, height, width = rows.shape
    capacity = count // counts.shape[0]
    out[:, :, width:] = jnp.full((count, height, DH), -1, BF)
    for g in range(counts.shape[0]):
        counts[g] = 0
    for i in range(count):
        slot = owner[i]
        position[i] = -1

        @pl.when(slot >= 0)
        def _(i=i, slot=slot):
            group = slot // slots_group
            place = group * capacity + counts[group]
            counts[group] += 1
            position[i] = place
            out[place, :, :width] = rows[i]
            tag = (slot - group * slots_group).astype(F32)
            out[place, :, width:] = jnp.full((height, DH), tag).astype(BF)


def pack(rows, hidden, grad, owner, groups, slots_group):
    count, height, width = rows.shape
    return pl.pallas_call(
        functools.partial(pack_kernel, slots_group),
        out_shape=(
            jax.ShapeDtypeStruct((count, height, width + DH), BF),
            jax.ShapeDtypeStruct((count,), jnp.int32),
            jax.ShapeDtypeStruct((2 * hidden.shape[0], hidden.shape[1]), BF),
        ),
        in_specs=[pl.BlockSpec(memory_space=pltpu.SMEM)] + in_vmem(3),
        out_specs=in_vmem(1) + [pl.BlockSpec(memory_space=pltpu.SMEM)] + in_vmem(1),
        scratch_shapes=[pltpu.SMEM((groups,), jnp.int32)],
        cost_estimate=pl.CostEstimate(
            flops=0, bytes_accessed=4 * math.prod(rows.shape), transcendentals=0
        ),
    )(owner, rows, hidden, grad)


def per_device(hidden_in, out_grad, neighbours, counts, slot_owner, w_query, w_key, w_value, w_out):
    groups = lax.axis_size("dp")
    spans = counts.shape[0]
    slots_group = spans * MAXN
    src_slots = slot_owner.shape[0]
    capacity = src_slots // groups
    reach = lax.axis_size("mp") // 4
    rows_dev = neighbours.shape[1]
    enc_width = neighbours.shape[2]
    tokens_dev = hidden_in.shape[0]
    span_len = tokens_dev // spans
    devices = lax.axis_size("mp")
    chips = devices // 2
    core = (lax.axis_index("mp") % 2).astype(jnp.int32)

    slot_order = jnp.arange(src_slots, dtype=jnp.int32)
    send_rows, position, both = pack(
        neighbours, hidden_in, out_grad, slot_owner, groups, slots_group
    )
    both = lax.all_gather(both, "mp", axis=1, tiled=True)
    got = lax.all_to_all(
        send_rows.reshape(groups, capacity, rows_dev, enc_width + DH),
        "dp",
        split_axis=0,
        concat_axis=0,
        tiled=True,
    ).reshape(src_slots, rows_dev, enc_width + DH)
    local_slot = got[:, 0, enc_width].astype(jnp.int32)
    slots = jnp.arange(slots_group, dtype=jnp.int32)
    wanted = (slots + core * MAXN) % slots_group
    matches = local_slot[None, :] == wanted[:, None]
    chosen = jnp.sum(jnp.where(matches, slot_order[None, :] + 1, 0), axis=1) - 1
    returns = jnp.maximum(jnp.where(core == 0, local_slot, (local_slot + MAXN) % slots_group), 0)
    chunk_rows = MAXN * rows_dev
    kept, given = pick(got, chosen, enc_width, spans)
    kept, given = kept.reshape(chunk_rows, enc_width), given.reshape(chunk_rows, enc_width)
    given = core_swap(given)
    w_key_partner, w_value_partner = core_swap(w_key), core_swap(w_value)
    pair = project(both, w_query, w_out)
    ups, downs = [kept, given], [kept, given]
    keys = [kept, given]
    for step in range(1, reach):
        ups, downs = ring_step(ups, downs)
        keys += ups + downs
    (ups, downs), pair = tie((ups, downs), pair)
    tokens = [
        lax.dynamic_slice_in_dim(pair, c * span_len, span_len, 0) for c in (core, 1 - core)
    ]
    lines = make_lines(
        tokens[0], core_swap(tokens[1]), (w_key, w_value, w_key_partner, w_value_partner)
    )
    keys += [chip_shift(ups[0], 1), chip_shift(downs[1], -1)]
    first_late = 2 + 4 * (reach - 2)
    early, late = keys[:first_late], keys[first_late:]

    count = lax.dynamic_slice_in_dim(counts, core, 1)
    shapes = [(chunk_rows, BF)] * len(keys)
    outs = make_softmax(
        count,
        lines,
        make_products(lines, early),
        late,
        rows_dev,
        shapes,
        1.0 / math.sqrt(DH),
    )
    weights, grads = outs[:2], outs[2:]
    attended, away = make_attended(weights, (w_value, w_value_partner), early, late, span_len)
    back = core_swap(away)
    attended = jnp.where(
        core == 0,
        jnp.concatenate([attended, back], axis=0),
        jnp.concatenate([back, attended], axis=0),
    )
    mine, other = project_out(core.reshape(1), attended, w_out, chips)
    sums = (mine + core_swap(other)).astype(BF)

    def part(distance, ring):
        return grads[4 * abs(distance) - 2 + (2 if distance > 0 else 0) + ring]

    chains = [
        (0, 1, reach, grads[-2]),
        (1, 1, reach - 1, part(reach - 1, 1)),
        (0, -1, reach - 1, part(1 - reach, 0)),
        (1, -1, reach, grads[-1]),
    ]
    scattered = [grads[0].astype(F32), grads[1].astype(F32)]
    for step in range(reach):
        if step == 2:
            values, mine = tie([chain[3] for chain in chains], mine)
            chains = [chain[:3] + (value,) for chain, value in zip(chains, values)]
        moved = []
        for ring, way, left, value in chains:
            value = chip_shift(value, way).astype(F32)
            if left > 1:
                value = (value + part(way * (left - 1), ring)).astype(BF)
                moved.append((ring, way, left - 1, value))
            else:
                scattered[ring] = scattered[ring] + value
        chains = moved
    scattered = to_bf16(scattered)
    grad_rows = jnp.concatenate([scattered[0], core_swap(scattered[1])], axis=0)
    grad_rows = grad_rows.reshape(slots_group, rows_dev, enc_width)

    layer_out = lax.psum_scatter(
        sums,
        "mp",
        scatter_dimension=0,
        axis_index_groups=[list(range(c, devices, 2)) for c in range(2)],
    )

    returned = lax.all_to_all(
        pick(grad_rows, returns)[0].reshape(groups, capacity, rows_dev, enc_width),
        "dp",
        split_axis=0,
        concat_axis=0,
        tiled=True,
    ).reshape(src_slots, rows_dev, enc_width)
    neighbour_grad = pick(returned, position)[0]
    return (layer_out, neighbour_grad)


def solution(mesh):
    return jax.shard_map(
        per_device,
        mesh=mesh,
        in_specs=(
            P("dp", "mp"),
            P("dp", "mp"),
            P("dp", "mp", None),
            P("dp"),
            P("dp"),
            P(None, "mp"),
            P(None, "mp"),
            P(None, "mp"),
            P("mp", None),
        ),
        out_specs=(P("dp", "mp"), P("dp", "mp", None)),
        check_vma=False,
    )
```

```python
import functools
import math

import jax
import jax.numpy as jnp
from jax import lax
from jax.experimental import pallas as pl
from jax.experimental.pallas import tpu as pltpu
from jax.sharding import PartitionSpec as P

DH = 128
MAXN = 10
BF = jnp.bfloat16
F32 = jnp.float32
LAST = (((1,), (1,)), ((), ()))
FIRST = (((0,), (0,)), ((), ()))


def dot(a, b):
    return jnp.dot(a, b, preferred_element_type=F32)


def dot_t(a, b):
    return lax.dot_general(a, b, LAST, preferred_element_type=F32)


def chip_shift(value, step):
    devices = lax.axis_size("mp")
    chips = devices // 2
    pairs = [
        (2 * z + c, 2 * ((z + step) % chips) + c) for z in range(chips) for c in range(2)
    ]
    return lax.ppermute(value, "mp", pairs)


def core_swap(value):
    return lax.ppermute(value, "mp", [(i, i ^ 1) for i in range(lax.axis_size("mp"))])


def after(values, first):
    return lax.optimization_barrier((values, first))[0]


def ring_step(ups, downs):
    return [chip_shift(u, 1) for u in ups], [chip_shift(d, -1) for d in downs]


def to_bf16(values):
    return [v.astype(BF) for v in values]


VMEM_LIMIT = 40 * 2**20


def in_vmem(count):
    return [pl.BlockSpec(memory_space=pltpu.VMEM)] * count


def out_kernel(core, attended, w_out, mine, other):
    width = w_out.shape[1] // 2
    parts = [dot(attended[...], w_out[:, i * width : (i + 1) * width]) for i in range(2)]
    first = core[0] == 0
    mine[0] = jnp.where(first, parts[0], parts[1])
    other[0] = jnp.where(first, parts[1], parts[0])


def project_out(core, attended, w_out, chips):
    tokens, features = attended.shape
    width = w_out.shape[1] // (2 * chips)
    out = jax.ShapeDtypeStruct((chips, tokens, width), F32)
    return pl.pallas_call(
        out_kernel,
        out_shape=(out, out),
        grid_spec=pltpu.PrefetchScalarGridSpec(
            num_scalar_prefetch=1,
            grid=(chips,),
            in_specs=[
                pl.BlockSpec((tokens, features), lambda i, p: (0, 0)),
                pl.BlockSpec((features, 2 * width), lambda i, p: (0, i)),
            ],
            out_specs=[
                pl.BlockSpec((1, tokens, width), lambda i, p: (i, 0, 0)),
                pl.BlockSpec((1, tokens, width), lambda i, p: (i, 0, 0)),
            ],
        ),
        compiler_params=pltpu.CompilerParams(vmem_limit_bytes=VMEM_LIMIT),
        cost_estimate=pl.CostEstimate(
            flops=4 * tokens * features * width * chips,
            bytes_accessed=4 * chips * width * (features + 4 * tokens),
            transcendentals=0,
        ),
    )(core, attended, w_out)


def lines_kernel(own, partner, key_own, value_own, key_partner, value_partner, lines):
    length, width = own.shape
    heads = width // (2 * DH)
    for kind, weights in enumerate(((key_own, key_partner), (value_own, value_partner))):
        for i, (pair, weight) in enumerate(zip((own, partner), weights)):
            for h in range(heads):
                part = slice((kind * heads + h) * DH, (kind * heads + h + 1) * DH)
                first = ((kind * 2 + i) * heads + h) * length
                made = dot_t(pair[:, part], weight[:, h * DH : (h + 1) * DH])
                high = made.astype(BF)
                lines[first : first + length] = high
                if kind == 0:
                    first += 4 * heads * length
                    lines[first : first + length] = (made - high.astype(F32)).astype(BF)


def make_lines(own, partner, weights):
    length, width = own.shape
    enc = weights[0].shape[0]
    rows = 3 * length * width // DH
    return pl.pallas_call(
        lines_kernel,
        out_shape=jax.ShapeDtypeStruct((rows, enc), BF),
        in_specs=in_vmem(6),
        out_specs=in_vmem(1)[0],
        compiler_params=pltpu.CompilerParams(vmem_limit_bytes=VMEM_LIMIT),
        cost_estimate=pl.CostEstimate(
            flops=2 * rows * DH * enc, bytes_accessed=4 * rows * enc, transcendentals=0
        ),
    )(own, partner, *weights)


def products_kernel(lines, *refs):
    keys = jnp.concatenate([r[...] for r in refs[:-1]], axis=0)
    refs[-1][...] = dot_t(lines[...], keys)


def make_products(lines, chunks):
    rows, enc = lines.shape
    count = sum(c.shape[0] for c in chunks)
    return pl.pallas_call(
        products_kernel,
        out_shape=jax.ShapeDtypeStruct((rows, count), F32),
        in_specs=in_vmem(1 + len(chunks)),
        out_specs=in_vmem(1)[0],
        compiler_params=pltpu.CompilerParams(vmem_limit_bytes=VMEM_LIMIT),
        cost_estimate=pl.CostEstimate(
            flops=2 * rows * count * enc,
            bytes_accessed=2 * enc * (rows + count) + 4 * rows * count,
            transcendentals=0,
        ),
    )(lines, *chunks)


def softmax_kernel(scale, per_slot, period, late, count, lines, early, *refs):
    keys = jnp.concatenate([r[...] for r in refs[:late]], axis=0)
    weights_out, grads_out = refs[late : late + 2], refs[late + 2 :]
    products = [early[...], dot_t(lines[...], keys)]
    middle = lines.shape[0] // 3
    scores = []
    for product in products:
        columns = lax.broadcasted_iota(jnp.int32, (middle, product.shape[1]), 1)
        live = (columns % period) // per_slot < count[0]
        score = (product[:middle] + product[2 * middle :]) * scale
        scores.append(jnp.where(live, score, -jnp.inf))
    peak = functools.reduce(
        jnp.maximum, [jnp.max(part, axis=-1, keepdims=True) for part in scores]
    )
    exponents = [jnp.exp(part - peak) for part in scores]
    total = sum(jnp.sum(part, axis=-1, keepdims=True) for part in exponents)
    weights = [part / total for part in exponents]
    inner = sum(
        jnp.sum(w * p[middle : 2 * middle], axis=-1, keepdims=True)
        for w, p in zip(weights, products)
    )
    place = 0
    for weight, product, out in zip(weights, products, weights_out):
        score = weight * (product[middle : 2 * middle] - inner) * scale
        rounded = weight.astype(BF)
        out[...] = rounded
        columns = jnp.concatenate([score.astype(BF), rounded], axis=0)
        made = lax.dot_general(
            columns, lines[: 2 * middle], FIRST, preferred_element_type=F32
        )
        first = 0
        while first < made.shape[0]:
            out = grads_out[place]
            out[...] = made[first : first + out.shape[0]].astype(out.dtype)
            first += out.shape[0]
            place += 1


def make_softmax(count, lines, early, chunks, per_slot, shapes, scale):
    rows, enc = lines.shape
    late = sum(c.shape[0] for c in chunks)
    keys = early.shape[1] + late
    period = shapes[0][0]
    return pl.pallas_call(
        functools.partial(softmax_kernel, scale, per_slot, period, len(chunks)),
        out_shape=[
            jax.ShapeDtypeStruct((rows // 3, early.shape[1]), BF),
            jax.ShapeDtypeStruct((rows // 3, late), BF),
        ]
        + [jax.ShapeDtypeStruct((n, enc), kind) for n, kind in shapes],
        in_specs=[pl.BlockSpec(memory_space=pltpu.SMEM)] + in_vmem(2 + len(chunks)),
        out_specs=in_vmem(2 + len(shapes)),
        compiler_params=pltpu.CompilerParams(vmem_limit_bytes=VMEM_LIMIT),
        cost_estimate=pl.CostEstimate(
            flops=2 * rows * (late + keys) * enc,
            bytes_accessed=2 * enc * (rows + late + 2 * keys) + 4 * rows * keys,
            transcendentals=rows * keys // 2,
        ),
    )(count, lines, early, *chunks)


def attended_kernel(early_count, first, second, value_own, value_partner, *refs):
    own, partner = refs[-2:]
    chunks = [r[...] for r in refs[:-2]]
    mixed = dot(first[...], jnp.concatenate(chunks[:early_count], axis=0))
    mixed += dot(second[...], jnp.concatenate(chunks[early_count:], axis=0))
    high = mixed.astype(BF)
    low = (mixed - high.astype(F32)).astype(BF)
    length, width = own.shape
    for i, (weight, out) in enumerate(((value_own, own), (value_partner, partner))):
        for h in range(width // DH):
            rows = slice((i * (width // DH) + h) * length, (i * (width // DH) + h + 1) * length)
            part = slice(h * DH, (h + 1) * DH)
            made = dot(high[rows], weight[:, part]) + dot(low[rows], weight[:, part])
            out[:, part] = made.astype(BF)


def make_attended(weights, values, early, late, length):
    rows, enc = weights[0].shape[0], values[0].shape[0]
    keys = weights[0].shape[1] + weights[1].shape[1]
    out = jax.ShapeDtypeStruct((length, values[0].shape[1]), BF)
    return pl.pallas_call(
        functools.partial(attended_kernel, len(early)),
        out_shape=(out, out),
        in_specs=in_vmem(4 + len(early) + len(late)),
        out_specs=in_vmem(2),
        compiler_params=pltpu.CompilerParams(vmem_limit_bytes=VMEM_LIMIT),
        cost_estimate=pl.CostEstimate(
            flops=2 * rows * keys * enc, bytes_accessed=2 * keys * (rows + enc), transcendentals=0
        ),
    )(*weights, *values, *early, *late)


def pick_kernel(parts, source, rows, *outs):
    count, _, width = outs[0].shape
    for i in range(count * parts):
        value = rows[jnp.maximum(source[i], 0), :, :width]
        outs[i // count][i % count] = jnp.where(source[i] >= 0, value, jnp.zeros_like(value))


def join_kernel(source, first, second, out):
    split = first.shape[0]
    for i in range(out.shape[0]):
        low = jnp.minimum(jnp.maximum(source[i], 0), split - 1)
        high = jnp.maximum(source[i] - split, 0)
        out[i] = jnp.where(source[i] < split, first[low], second[high])


def join_pick(first, second, source):
    shape = (source.shape[0],) + first.shape[1:]
    return pl.pallas_call(
        join_kernel,
        out_shape=jax.ShapeDtypeStruct(shape, BF),
        in_specs=[pl.BlockSpec(memory_space=pltpu.SMEM)] + in_vmem(2),
        out_specs=in_vmem(1)[0],
        cost_estimate=pl.CostEstimate(
            flops=0, bytes_accessed=4 * math.prod(shape), transcendentals=0
        ),
    )(source.astype(jnp.int32), first, second)


def pick(rows, source, width=None, parts=1):
    shape = (source.shape[0] // parts, rows.shape[1], width or rows.shape[2])
    return pl.pallas_call(
        functools.partial(pick_kernel, parts),
        out_shape=[jax.ShapeDtypeStruct(shape, BF)] * parts,
        in_specs=[pl.BlockSpec(memory_space=pltpu.SMEM)] + in_vmem(1),
        out_specs=in_vmem(parts),
        cost_estimate=pl.CostEstimate(
            flops=0, bytes_accessed=4 * parts * math.prod(shape), transcendentals=0
        ),
    )(source.astype(jnp.int32), rows)


def pack_kernel(slots_group, owner, rows, hidden, grad, out, position, both, counts):
    both[: hidden.shape[0]] = hidden[...]
    both[hidden.shape[0] :] = grad[...]
    count, height, width = rows.shape
    capacity = count // counts.shape[0]
    out[:, :, width:] = jnp.full((count, height, DH), -1, BF)
    for g in range(counts.shape[0]):
        counts[g] = 0
    for i in range(count):
        slot = owner[i]
        position[i] = -1

        @pl.when(slot >= 0)
        def _(i=i, slot=slot):
            group = slot // slots_group
            place = group * capacity + counts[group]
            counts[group] += 1
            position[i] = place
            out[place, :, :width] = rows[i]
            tag = (slot - group * slots_group).astype(F32)
            out[place, :, width:] = jnp.full((height, DH), tag).astype(BF)


def pack(rows, hidden, grad, owner, groups, slots_group):
    count, height, width = rows.shape
    return pl.pallas_call(
        functools.partial(pack_kernel, slots_group),
        out_shape=(
            jax.ShapeDtypeStruct((count, height, width + DH), BF),
            jax.ShapeDtypeStruct((count,), jnp.int32),
            jax.ShapeDtypeStruct((2 * hidden.shape[0], hidden.shape[1]), BF),
        ),
        in_specs=[pl.BlockSpec(memory_space=pltpu.SMEM)] + in_vmem(3),
        out_specs=in_vmem(1) + [pl.BlockSpec(memory_space=pltpu.SMEM)] + in_vmem(1),
        scratch_shapes=[pltpu.SMEM((groups,), jnp.int32)],
        cost_estimate=pl.CostEstimate(
            flops=0, bytes_accessed=4 * math.prod(rows.shape), transcendentals=0
        ),
    )(owner, rows, hidden, grad)


def per_device(hidden_in, out_grad, neighbours, counts, slot_owner, w_query, w_key, w_value, w_out):
    groups = lax.axis_size("dp")
    spans = counts.shape[0]
    slots_group = spans * MAXN
    src_slots = slot_owner.shape[0]
    capacity = src_slots // groups
    reach = lax.axis_size("mp") // 4
    rows_dev = neighbours.shape[1]
    enc_width = neighbours.shape[2]
    tokens_dev = hidden_in.shape[0]
    span_len = tokens_dev // spans
    devices = lax.axis_size("mp")
    chips = devices // 2
    core = (lax.axis_index("mp") % 2).astype(jnp.int32)

    slot_order = jnp.arange(src_slots, dtype=jnp.int32)
    send_rows, position, both = pack(
        neighbours, hidden_in, out_grad, slot_owner, groups, slots_group
    )
    both = lax.all_gather(both, "mp", axis=1, tiled=True)
    got = lax.all_to_all(
        send_rows.reshape(groups, capacity, rows_dev, enc_width + DH),
        "dp",
        split_axis=0,
        concat_axis=0,
        tiled=True,
    ).reshape(src_slots, rows_dev, enc_width + DH)
    local_slot = got[:, 0, enc_width].astype(jnp.int32)
    slots = jnp.arange(slots_group, dtype=jnp.int32)
    wanted = (slots + core * MAXN) % slots_group
    matches = local_slot[None, :] == wanted[:, None]
    chosen = jnp.sum(jnp.where(matches, slot_order[None, :] + 1, 0), axis=1) - 1
    returns = jnp.maximum(jnp.where(core == 0, local_slot, (local_slot + MAXN) % slots_group), 0)
    chunk_rows = MAXN * rows_dev
    kept, given = pick(got, chosen, enc_width, spans)
    kept, given = kept.reshape(chunk_rows, enc_width), given.reshape(chunk_rows, enc_width)
    given = core_swap(given)
    w_key_partner, w_value_partner = core_swap(w_key), core_swap(w_value)
    queries = dot(both[:tokens_dev], w_query).astype(BF)
    grad_attended = dot_t(both[tokens_dev:], w_out).astype(BF)
    pair = jnp.concatenate([queries, grad_attended], axis=1)
    ups, downs = [kept, given], [kept, given]
    keys = [kept, given]
    for step in range(1, reach):
        ups, downs = ring_step(ups, downs)
        keys += ups + downs
    tokens = [
        lax.dynamic_slice_in_dim(pair, c * span_len, span_len, 0) for c in (core, 1 - core)
    ]
    lines = make_lines(
        tokens[0], core_swap(tokens[1]), (w_key, w_value, w_key_partner, w_value_partner)
    )
    ups[0], downs[1] = after([ups[0], downs[1]], lines)
    keys += [chip_shift(ups[0], 1), chip_shift(downs[1], -1)]
    first_late = 2 + 4 * (reach - 2)
    early, late = keys[:first_late], keys[first_late:]

    count = lax.dynamic_slice_in_dim(counts, core, 1)
    shapes = [(chunk_rows, BF)] * len(keys)
    outs = make_softmax(
        count,
        lines,
        make_products(lines, early),
        late,
        rows_dev,
        shapes,
        1.0 / math.sqrt(DH),
    )
    weights, grads = outs[:2], outs[2:]
    attended, away = make_attended(weights, (w_value, w_value_partner), early, late, span_len)
    back = core_swap(away)
    attended = jnp.where(
        core == 0,
        jnp.concatenate([attended, back], axis=0),
        jnp.concatenate([back, attended], axis=0),
    )
    mine, other = project_out(core.reshape(1), attended, w_out, chips)
    sums = (mine + core_swap(other)).astype(BF)

    def part(distance, ring):
        return grads[4 * abs(distance) - 2 + (2 if distance > 0 else 0) + ring]

    chains = [
        (0, 1, reach, grads[-2]),
        (1, 1, reach - 1, part(reach - 1, 1)),
        (0, -1, reach - 1, part(1 - reach, 0)),
        (1, -1, reach, grads[-1]),
    ]
    scattered = [grads[0].astype(F32), grads[1].astype(F32)]
    for step in range(reach):
        moved = []
        for ring, way, left, value in chains:
            value = chip_shift(value, way).astype(F32)
            if left > 1:
                value = (value + part(way * (left - 1), ring)).astype(BF)
                moved.append((ring, way, left - 1, value))
            else:
                scattered[ring] = scattered[ring] + value
        chains = moved
    scattered = to_bf16(scattered)
    scattered[1] = core_swap(scattered[1])
    scattered = [part.reshape(MAXN, rows_dev, enc_width) for part in scattered]

    layer_out = lax.psum_scatter(
        sums,
        "mp",
        scatter_dimension=0,
        axis_index_groups=[list(range(c, devices, 2)) for c in range(2)],
    )

    returned = lax.all_to_all(
        join_pick(*scattered, returns).reshape(groups, capacity, rows_dev, enc_width),
        "dp",
        split_axis=0,
        concat_axis=0,
        tiled=True,
    ).reshape(src_slots, rows_dev, enc_width)
    neighbour_grad = pick(returned, position)[0]
    return (layer_out, neighbour_grad)


def solution(mesh):
    return jax.shard_map(
        per_device,
        mesh=mesh,
        in_specs=(
            P("dp", "mp"),
            P("dp", "mp"),
            P("dp", "mp", None),
            P("dp"),
            P("dp"),
            P(None, "mp"),
            P(None, "mp"),
            P(None, "mp"),
            P("mp", None),
        ),
        out_specs=(P("dp", "mp"), P("dp", "mp", None)),
        check_vma=False,
    )
```

```python
import functools
import math

import jax
import jax.numpy as jnp
from jax import lax
from jax.experimental import pallas as pl
from jax.experimental.pallas import tpu as pltpu
from jax.sharding import PartitionSpec as P

DH = 128
MAXN = 10
BF = jnp.bfloat16
F32 = jnp.float32
LAST = (((1,), (1,)), ((), ()))
FIRST = (((0,), (0,)), ((), ()))


def dot(a, b):
    return jnp.dot(a, b, preferred_element_type=F32)


def dot_t(a, b):
    return lax.dot_general(a, b, LAST, preferred_element_type=F32)


def chip_shift(value, step):
    devices = lax.axis_size("mp")
    chips = devices // 2
    pairs = [
        (2 * z + c, 2 * ((z + step) % chips) + c) for z in range(chips) for c in range(2)
    ]
    return lax.ppermute(value, "mp", pairs)


def core_swap(value):
    return lax.ppermute(value, "mp", [(i, i ^ 1) for i in range(lax.axis_size("mp"))])


def after(values, first):
    return lax.optimization_barrier((values, first))[0]


def ring_step(ups, downs):
    return [chip_shift(u, 1) for u in ups], [chip_shift(d, -1) for d in downs]


def to_bf16(values):
    return [v.astype(BF) for v in values]


VMEM_LIMIT = 40 * 2**20


def in_vmem(count):
    return [pl.BlockSpec(memory_space=pltpu.VMEM)] * count


def out_kernel(core, attended, w_out, mine, other):
    width = w_out.shape[1] // 2
    parts = [dot(attended[...], w_out[:, i * width : (i + 1) * width]) for i in range(2)]
    first = core[0] == 0
    mine[0] = jnp.where(first, parts[0], parts[1])
    other[0] = jnp.where(first, parts[1], parts[0])


def project_out(core, attended, w_out, chips):
    tokens, features = attended.shape
    width = w_out.shape[1] // (2 * chips)
    out = jax.ShapeDtypeStruct((chips, tokens, width), F32)
    return pl.pallas_call(
        out_kernel,
        out_shape=(out, out),
        grid_spec=pltpu.PrefetchScalarGridSpec(
            num_scalar_prefetch=1,
            grid=(chips,),
            in_specs=[
                pl.BlockSpec((tokens, features), lambda i, p: (0, 0)),
                pl.BlockSpec((features, 2 * width), lambda i, p: (0, i)),
            ],
            out_specs=[
                pl.BlockSpec((1, tokens, width), lambda i, p: (i, 0, 0)),
                pl.BlockSpec((1, tokens, width), lambda i, p: (i, 0, 0)),
            ],
        ),
        compiler_params=pltpu.CompilerParams(vmem_limit_bytes=VMEM_LIMIT),
        cost_estimate=pl.CostEstimate(
            flops=4 * tokens * features * width * chips,
            bytes_accessed=4 * chips * width * (features + 4 * tokens),
            transcendentals=0,
        ),
    )(core, attended, w_out)


def lines_kernel(own, partner, key_own, value_own, key_partner, value_partner, lines):
    length, width = own.shape
    heads = width // (2 * DH)
    for kind, weights in enumerate(((key_own, key_partner), (value_own, value_partner))):
        for i, (pair, weight) in enumerate(zip((own, partner), weights)):
            for h in range(heads):
                part = slice((kind * heads + h) * DH, (kind * heads + h + 1) * DH)
                first = ((kind * 2 + i) * heads + h) * length
                made = dot_t(pair[:, part], weight[:, h * DH : (h + 1) * DH])
                high = made.astype(BF)
                lines[first : first + length] = high
                if kind == 0:
                    first += 4 * heads * length
                    lines[first : first + length] = (made - high.astype(F32)).astype(BF)


def make_lines(own, partner, weights):
    length, width = own.shape
    enc = weights[0].shape[0]
    rows = 3 * length * width // DH
    return pl.pallas_call(
        lines_kernel,
        out_shape=jax.ShapeDtypeStruct((rows, enc), BF),
        in_specs=in_vmem(6),
        out_specs=in_vmem(1)[0],
        compiler_params=pltpu.CompilerParams(vmem_limit_bytes=VMEM_LIMIT),
        cost_estimate=pl.CostEstimate(
            flops=2 * rows * DH * enc, bytes_accessed=4 * rows * enc, transcendentals=0
        ),
    )(own, partner, *weights)


def gather(refs, keys):
    first = 0
    for ref in refs:
        keys[first : first + ref.shape[0]] = ref[...]
        first += ref.shape[0]


def products(lines, keys, out):
    step = 2 * DH

    @pl.loop(0, lines.shape[0] // step)
    def _(i):
        rows = pl.ds(pl.multiple_of(i * step, step), step)
        out[rows] = dot_t(lines[rows], keys[...])


def products_kernel(lines, *refs):
    out, keys = refs[-2:]
    gather(refs[:-2], keys)
    products(lines, keys, out)


def make_products(lines, chunks):
    rows, enc = lines.shape
    count = sum(c.shape[0] for c in chunks)
    return pl.pallas_call(
        products_kernel,
        out_shape=jax.ShapeDtypeStruct((rows, count), F32),
        in_specs=in_vmem(1 + len(chunks)),
        out_specs=in_vmem(1)[0],
        scratch_shapes=[pltpu.VMEM((count, enc), BF)],
        compiler_params=pltpu.CompilerParams(vmem_limit_bytes=VMEM_LIMIT),
        cost_estimate=pl.CostEstimate(
            flops=2 * rows * count * enc,
            bytes_accessed=2 * enc * (rows + count) + 4 * rows * count,
            transcendentals=0,
        ),
    )(lines, *chunks)


def softmax_kernel(scale, per_slot, period, late, count, lines, early, *refs):
    keys, last, *columns_refs = refs[-4:]
    weights_out, grads_out = refs[late : late + 2], refs[late + 2 : -4]
    gather(refs[:late], keys)
    products(lines, keys, last)
    both = [early[...], last[...]]
    middle = lines.shape[0] // 3
    scores = []
    for product in both:
        columns = lax.broadcasted_iota(jnp.int32, (middle, product.shape[1]), 1)
        live = (columns % period) // per_slot < count[0]
        score = (product[:middle] + product[2 * middle :]) * scale
        scores.append(jnp.where(live, score, -jnp.inf))
    peak = functools.reduce(
        jnp.maximum, [jnp.max(part, axis=-1, keepdims=True) for part in scores]
    )
    exponents = [jnp.exp(part - peak) for part in scores]
    total = sum(jnp.sum(part, axis=-1, keepdims=True) for part in exponents)
    weights = [part / total for part in exponents]
    inner = sum(
        jnp.sum(w * p[middle : 2 * middle], axis=-1, keepdims=True)
        for w, p in zip(weights, both)
    )
    for weight, product, out, columns in zip(weights, both, weights_out, columns_refs):
        score = weight * (product[middle : 2 * middle] - inner) * scale
        rounded = weight.astype(BF)
        out[...] = rounded
        columns[:middle] = score.astype(BF)
        columns[middle:] = rounded
    step = 4 * DH

    @pl.loop(0, lines.shape[1] // step)
    def _(i):
        part = pl.ds(pl.multiple_of(i * step, step), step)
        right = lines[: 2 * middle, part]
        place = 0
        for columns in columns_refs:
            made = lax.dot_general(columns[...], right, FIRST, preferred_element_type=F32)
            first = 0
            while first < made.shape[0]:
                out = grads_out[place]
                out[:, part] = made[first : first + out.shape[0]].astype(out.dtype)
                first += out.shape[0]
                place += 1


def make_softmax(count, lines, early, chunks, per_slot, shapes, scale):
    rows, enc = lines.shape
    late = sum(c.shape[0] for c in chunks)
    keys = early.shape[1] + late
    period = shapes[0][0]
    return pl.pallas_call(
        functools.partial(softmax_kernel, scale, per_slot, period, len(chunks)),
        out_shape=[
            jax.ShapeDtypeStruct((rows // 3, early.shape[1]), BF),
            jax.ShapeDtypeStruct((rows // 3, late), BF),
        ]
        + [jax.ShapeDtypeStruct((n, enc), kind) for n, kind in shapes],
        in_specs=[pl.BlockSpec(memory_space=pltpu.SMEM)] + in_vmem(2 + len(chunks)),
        out_specs=in_vmem(2 + len(shapes)),
        scratch_shapes=[
            pltpu.VMEM((late, enc), BF),
            pltpu.VMEM((rows, late), F32),
            pltpu.VMEM((rows // 3 * 2, early.shape[1]), BF),
            pltpu.VMEM((rows // 3 * 2, late), BF),
        ],
        compiler_params=pltpu.CompilerParams(vmem_limit_bytes=VMEM_LIMIT),
        cost_estimate=pl.CostEstimate(
            flops=2 * rows * (late + keys) * enc,
            bytes_accessed=2 * enc * (rows + late + 2 * keys) + 4 * rows * keys,
            transcendentals=rows * keys // 2,
        ),
    )(count, lines, early, *chunks)


def attended_kernel(first, second, value_own, value_partner, *refs):
    own, partner, keys, high, low = refs[-5:]
    gather(refs[:-5], keys)
    split, step = first.shape[1], 4 * DH

    @pl.loop(0, keys.shape[1] // step)
    def _(i):
        part = pl.ds(pl.multiple_of(i * step, step), step)
        mixed = dot(first[...], keys[:split, part]) + dot(second[...], keys[split:, part])
        rounded = mixed.astype(BF)
        high[:, part] = rounded
        low[:, part] = (mixed - rounded.astype(F32)).astype(BF)

    length, width = own.shape
    for i, (weight, out) in enumerate(((value_own, own), (value_partner, partner))):
        for h in range(width // DH):
            rows = slice((i * (width // DH) + h) * length, (i * (width // DH) + h + 1) * length)
            part = slice(h * DH, (h + 1) * DH)
            made = dot(high[rows], weight[:, part]) + dot(low[rows], weight[:, part])
            out[:, part] = made.astype(BF)


def make_attended(weights, values, early, late, length):
    rows, enc = weights[0].shape[0], values[0].shape[0]
    keys = weights[0].shape[1] + weights[1].shape[1]
    out = jax.ShapeDtypeStruct((length, values[0].shape[1]), BF)
    return pl.pallas_call(
        attended_kernel,
        out_shape=(out, out),
        in_specs=in_vmem(4 + len(early) + len(late)),
        out_specs=in_vmem(2),
        scratch_shapes=[pltpu.VMEM((n, enc), BF) for n in (keys, rows, rows)],
        compiler_params=pltpu.CompilerParams(vmem_limit_bytes=VMEM_LIMIT),
        cost_estimate=pl.CostEstimate(
            flops=2 * rows * keys * enc, bytes_accessed=2 * keys * (rows + enc), transcendentals=0
        ),
    )(*weights, *values, *early, *late)


def pick_kernel(parts, source, rows, *outs):
    count, _, width = outs[0].shape
    for k in range(parts):

        @pl.loop(0, count)
        def _(i, k=k):
            index = source[k * count + i]
            value = rows[jnp.maximum(index, 0), :, :width]
            outs[k][i] = jnp.where(index >= 0, value, jnp.zeros_like(value))


def join_kernel(source, first, second, out):
    split = first.shape[0]

    @pl.loop(0, out.shape[0])
    def _(i):
        low = jnp.minimum(jnp.maximum(source[i], 0), split - 1)
        high = jnp.maximum(source[i] - split, 0)
        out[i] = jnp.where(source[i] < split, first[low], second[high])


def join_pick(first, second, source):
    shape = (source.shape[0],) + first.shape[1:]
    return pl.pallas_call(
        join_kernel,
        out_shape=jax.ShapeDtypeStruct(shape, BF),
        in_specs=[pl.BlockSpec(memory_space=pltpu.SMEM)] + in_vmem(2),
        out_specs=in_vmem(1)[0],
        cost_estimate=pl.CostEstimate(
            flops=0, bytes_accessed=4 * math.prod(shape), transcendentals=0
        ),
    )(source.astype(jnp.int32), first, second)


def pick(rows, source, width=None, parts=1):
    shape = (source.shape[0] // parts, rows.shape[1], width or rows.shape[2])
    return pl.pallas_call(
        functools.partial(pick_kernel, parts),
        out_shape=[jax.ShapeDtypeStruct(shape, BF)] * parts,
        in_specs=[pl.BlockSpec(memory_space=pltpu.SMEM)] + in_vmem(1),
        out_specs=in_vmem(parts),
        cost_estimate=pl.CostEstimate(
            flops=0, bytes_accessed=4 * parts * math.prod(shape), transcendentals=0
        ),
    )(source.astype(jnp.int32), rows)


def pack_kernel(slots_group, owner, rows, hidden, grad, out, position, both, counts):
    both[: hidden.shape[0]] = hidden[...]
    both[hidden.shape[0] :] = grad[...]
    count, height, width = rows.shape
    capacity = count // counts.shape[0]
    out[:, :, width:] = jnp.full((count, height, DH), -1, BF)
    for g in range(counts.shape[0]):
        counts[g] = 0

    @pl.loop(0, count)
    def _(i):
        slot = owner[i]
        position[i] = -1

        @pl.when(slot >= 0)
        def _():
            group = slot // slots_group
            place = group * capacity + counts[group]
            counts[group] += 1
            position[i] = place
            out[place, :, :width] = rows[i]
            tag = (slot - group * slots_group).astype(F32)
            out[place, :, width:] = jnp.full((height, DH), tag).astype(BF)


def pack(rows, hidden, grad, owner, groups, slots_group):
    count, height, width = rows.shape
    return pl.pallas_call(
        functools.partial(pack_kernel, slots_group),
        out_shape=(
            jax.ShapeDtypeStruct((count, height, width + DH), BF),
            jax.ShapeDtypeStruct((count,), jnp.int32),
            jax.ShapeDtypeStruct((2 * hidden.shape[0], hidden.shape[1]), BF),
        ),
        in_specs=[pl.BlockSpec(memory_space=pltpu.SMEM)] + in_vmem(3),
        out_specs=in_vmem(1) + [pl.BlockSpec(memory_space=pltpu.SMEM)] + in_vmem(1),
        scratch_shapes=[pltpu.SMEM((groups,), jnp.int32)],
        cost_estimate=pl.CostEstimate(
            flops=0, bytes_accessed=4 * math.prod(rows.shape), transcendentals=0
        ),
    )(owner, rows, hidden, grad)


def per_device(hidden_in, out_grad, neighbours, counts, slot_owner, w_query, w_key, w_value, w_out):
    groups = lax.axis_size("dp")
    spans = counts.shape[0]
    slots_group = spans * MAXN
    src_slots = slot_owner.shape[0]
    capacity = src_slots // groups
    reach = lax.axis_size("mp") // 4
    rows_dev = neighbours.shape[1]
    enc_width = neighbours.shape[2]
    tokens_dev = hidden_in.shape[0]
    span_len = tokens_dev // spans
    devices = lax.axis_size("mp")
    chips = devices // 2
    core = (lax.axis_index("mp") % 2).astype(jnp.int32)

    slot_order = jnp.arange(src_slots, dtype=jnp.int32)
    send_rows, position, both = pack(
        neighbours, hidden_in, out_grad, slot_owner, groups, slots_group
    )
    both = lax.all_gather(both, "mp", axis=1, tiled=True)
    got = lax.all_to_all(
        send_rows.reshape(groups, capacity, rows_dev, enc_width + DH),
        "dp",
        split_axis=0,
        concat_axis=0,
        tiled=True,
    ).reshape(src_slots, rows_dev, enc_width + DH)
    local_slot = got[:, 0, enc_width].astype(jnp.int32)
    slots = jnp.arange(slots_group, dtype=jnp.int32)
    wanted = (slots + core * MAXN) % slots_group
    matches = local_slot[None, :] == wanted[:, None]
    chosen = jnp.sum(jnp.where(matches, slot_order[None, :] + 1, 0), axis=1) - 1
    returns = jnp.maximum(jnp.where(core == 0, local_slot, (local_slot + MAXN) % slots_group), 0)
    chunk_rows = MAXN * rows_dev
    kept, given = pick(got, chosen, enc_width, spans)
    kept, given = kept.reshape(chunk_rows, enc_width), given.reshape(chunk_rows, enc_width)
    given = core_swap(given)
    w_key_partner, w_value_partner = core_swap(w_key), core_swap(w_value)
    queries = dot(both[:tokens_dev], w_query).astype(BF)
    grad_attended = dot_t(both[tokens_dev:], w_out).astype(BF)
    pair = jnp.concatenate([queries, grad_attended], axis=1)
    ups, downs = [kept, given], [kept, given]
    keys = [kept, given]
    for step in range(1, reach):
        ups, downs = ring_step(ups, downs)
        keys += ups + downs
    tokens = [
        lax.dynamic_slice_in_dim(pair, c * span_len, span_len, 0) for c in (core, 1 - core)
    ]
    lines = make_lines(
        tokens[0], core_swap(tokens[1]), (w_key, w_value, w_key_partner, w_value_partner)
    )
    ups[0], downs[1] = after([ups[0], downs[1]], lines)
    keys += [chip_shift(ups[0], 1), chip_shift(downs[1], -1)]
    first_late = 2 + 4 * (reach - 2)
    early, late = keys[:first_late], keys[first_late:]

    count = lax.dynamic_slice_in_dim(counts, core, 1)
    shapes = [(chunk_rows, BF)] * len(keys)
    outs = make_softmax(
        count,
        lines,
        make_products(lines, early),
        late,
        rows_dev,
        shapes,
        1.0 / math.sqrt(DH),
    )
    weights, grads = outs[:2], outs[2:]
    attended, away = make_attended(weights, (w_value, w_value_partner), early, late, span_len)
    back = core_swap(away)
    attended = jnp.where(
        core == 0,
        jnp.concatenate([attended, back], axis=0),
        jnp.concatenate([back, attended], axis=0),
    )
    mine, other = project_out(core.reshape(1), attended, w_out, chips)
    sums = (mine + core_swap(other)).astype(BF)

    def part(distance, ring):
        return grads[4 * abs(distance) - 2 + (2 if distance > 0 else 0) + ring]

    chains = [
        (0, 1, reach, grads[-2]),
        (1, 1, reach - 1, part(reach - 1, 1)),
        (0, -1, reach - 1, part(1 - reach, 0)),
        (1, -1, reach, grads[-1]),
    ]
    scattered = [grads[0].astype(F32), grads[1].astype(F32)]
    for step in range(reach):
        moved = []
        for ring, way, left, value in chains:
            value = chip_shift(value, way).astype(F32)
            if left > 1:
                value = (value + part(way * (left - 1), ring)).astype(BF)
                moved.append((ring, way, left - 1, value))
            else:
                scattered[ring] = scattered[ring] + value
        chains = moved
    scattered = to_bf16(scattered)
    scattered[1] = core_swap(scattered[1])
    scattered = [part.reshape(MAXN, rows_dev, enc_width) for part in scattered]

    layer_out = lax.psum_scatter(
        sums,
        "mp",
        scatter_dimension=0,
        axis_index_groups=[list(range(c, devices, 2)) for c in range(2)],
    )

    returned = lax.all_to_all(
        join_pick(*scattered, returns).reshape(groups, capacity, rows_dev, enc_width),
        "dp",
        split_axis=0,
        concat_axis=0,
        tiled=True,
    ).reshape(src_slots, rows_dev, enc_width)
    neighbour_grad = pick(returned, position)[0]
    return (layer_out, neighbour_grad)


def solution(mesh):
    return jax.shard_map(
        per_device,
        mesh=mesh,
        in_specs=(
            P("dp", "mp"),
            P("dp", "mp"),
            P("dp", "mp", None),
            P("dp"),
            P("dp"),
            P(None, "mp"),
            P(None, "mp"),
            P(None, "mp"),
            P("mp", None),
        ),
        out_specs=(P("dp", "mp"), P("dp", "mp", None)),
        check_vma=False,
    )
```

```python
import functools
import math

import jax
import jax.numpy as jnp
from jax import lax
from jax.experimental import pallas as pl
from jax.experimental.pallas import tpu as pltpu
from jax.sharding import PartitionSpec as P

DH = 128
MAXN = 10
BF = jnp.bfloat16
F32 = jnp.float32
LAST = (((1,), (1,)), ((), ()))
FIRST = (((0,), (0,)), ((), ()))


def dot(a, b):
    return jnp.dot(a, b, preferred_element_type=F32)


def dot_t(a, b):
    return lax.dot_general(a, b, LAST, preferred_element_type=F32)


def chip_shift(value, step):
    devices = lax.axis_size("mp")
    chips = devices // 2
    pairs = [
        (2 * z + c, 2 * ((z + step) % chips) + c) for z in range(chips) for c in range(2)
    ]
    return lax.ppermute(value, "mp", pairs)


def core_swap(value):
    return lax.ppermute(value, "mp", [(i, i ^ 1) for i in range(lax.axis_size("mp"))])


def after(values, first):
    return lax.optimization_barrier((values, first))[0]


def ring_step(ups, downs):
    return [chip_shift(u, 1) for u in ups], [chip_shift(d, -1) for d in downs]


def to_bf16(values):
    return [v.astype(BF) for v in values]


VMEM_LIMIT = 40 * 2**20


def in_vmem(count):
    return [pl.BlockSpec(memory_space=pltpu.VMEM)] * count


def out_kernel(core, attended, w_out, mine, other):
    width = w_out.shape[1] // 2
    parts = [dot(attended[...], w_out[:, i * width : (i + 1) * width]) for i in range(2)]
    first = core[0] == 0
    mine[0] = jnp.where(first, parts[0], parts[1])
    other[0] = jnp.where(first, parts[1], parts[0])


def project_out(core, attended, w_out, chips):
    tokens, features = attended.shape
    width = w_out.shape[1] // (2 * chips)
    out = jax.ShapeDtypeStruct((chips, tokens, width), F32)
    return pl.pallas_call(
        out_kernel,
        out_shape=(out, out),
        grid_spec=pltpu.PrefetchScalarGridSpec(
            num_scalar_prefetch=1,
            grid=(chips,),
            in_specs=[
                pl.BlockSpec((tokens, features), lambda i, p: (0, 0)),
                pl.BlockSpec((features, 2 * width), lambda i, p: (0, i)),
            ],
            out_specs=[
                pl.BlockSpec((1, tokens, width), lambda i, p: (i, 0, 0)),
                pl.BlockSpec((1, tokens, width), lambda i, p: (i, 0, 0)),
            ],
        ),
        compiler_params=pltpu.CompilerParams(vmem_limit_bytes=VMEM_LIMIT),
        cost_estimate=pl.CostEstimate(
            flops=4 * tokens * features * width * chips,
            bytes_accessed=4 * chips * width * (features + 4 * tokens),
            transcendentals=0,
        ),
    )(core, attended, w_out)


def lines_kernel(own, partner, key_own, value_own, key_partner, value_partner, lines):
    length, width = own.shape
    heads = width // (2 * DH)
    for kind, weights in enumerate(((key_own, key_partner), (value_own, value_partner))):
        for i, (pair, weight) in enumerate(zip((own, partner), weights)):
            for h in range(heads):
                part = slice((kind * heads + h) * DH, (kind * heads + h + 1) * DH)
                first = ((kind * 2 + i) * heads + h) * length
                made = dot_t(pair[:, part], weight[:, h * DH : (h + 1) * DH])
                high = made.astype(BF)
                lines[first : first + length] = high
                if kind == 0:
                    first += 4 * heads * length
                    lines[first : first + length] = (made - high.astype(F32)).astype(BF)


def make_lines(own, partner, weights):
    length, width = own.shape
    enc = weights[0].shape[0]
    rows = 3 * length * width // DH
    return pl.pallas_call(
        lines_kernel,
        out_shape=jax.ShapeDtypeStruct((rows, enc), BF),
        in_specs=in_vmem(6),
        out_specs=in_vmem(1)[0],
        compiler_params=pltpu.CompilerParams(vmem_limit_bytes=VMEM_LIMIT),
        cost_estimate=pl.CostEstimate(
            flops=2 * rows * DH * enc, bytes_accessed=4 * rows * enc, transcendentals=0
        ),
    )(own, partner, *weights)


def gather(refs, keys):
    first = 0
    for ref in refs:
        keys[first : first + ref.shape[0]] = ref[...]
        first += ref.shape[0]


def products(lines, keys, out):
    step = 2 * DH

    @pl.loop(0, lines.shape[0] // step)
    def _(i):
        rows = pl.ds(pl.multiple_of(i * step, step), step)
        out[rows] = dot_t(lines[rows], keys[...])


def products_kernel(lines, *refs):
    out, keys = refs[-2:]
    gather(refs[:-2], keys)
    products(lines, keys, out)


def make_products(lines, chunks):
    rows, enc = lines.shape
    count = sum(c.shape[0] for c in chunks)
    return pl.pallas_call(
        products_kernel,
        out_shape=jax.ShapeDtypeStruct((rows, count), F32),
        in_specs=in_vmem(1 + len(chunks)),
        out_specs=in_vmem(1)[0],
        scratch_shapes=[pltpu.VMEM((count, enc), BF)],
        compiler_params=pltpu.CompilerParams(vmem_limit_bytes=VMEM_LIMIT),
        cost_estimate=pl.CostEstimate(
            flops=2 * rows * count * enc,
            bytes_accessed=2 * enc * (rows + count) + 4 * rows * count,
            transcendentals=0,
        ),
    )(lines, *chunks)


def softmax_kernel(scale, per_slot, period, late, core, counts, lines, early, *refs):
    keys, last, *columns_refs = refs[-4:]
    weights_out, grads_out = refs[late : late + 2], refs[late + 2 : -4]
    gather(refs[:late], keys)
    products(lines, keys, last)
    both = [early[...], last[...]]
    middle = lines.shape[0] // 3
    scores = []
    for product in both:
        columns = lax.broadcasted_iota(jnp.int32, (middle, product.shape[1]), 1)
        live = (columns % period) // per_slot < counts[core[0]]
        score = (product[:middle] + product[2 * middle :]) * scale
        scores.append(jnp.where(live, score, -jnp.inf))
    peak = functools.reduce(
        jnp.maximum, [jnp.max(part, axis=-1, keepdims=True) for part in scores]
    )
    exponents = [jnp.exp(part - peak) for part in scores]
    total = sum(jnp.sum(part, axis=-1, keepdims=True) for part in exponents)
    weights = [part / total for part in exponents]
    inner = sum(
        jnp.sum(w * p[middle : 2 * middle], axis=-1, keepdims=True)
        for w, p in zip(weights, both)
    )
    for weight, product, out, columns in zip(weights, both, weights_out, columns_refs):
        score = weight * (product[middle : 2 * middle] - inner) * scale
        rounded = weight.astype(BF)
        out[...] = rounded
        columns[:middle] = score.astype(BF)
        columns[middle:] = rounded
    step = 4 * DH

    @pl.loop(0, lines.shape[1] // step)
    def _(i):
        part = pl.ds(pl.multiple_of(i * step, step), step)
        right = lines[: 2 * middle, part]
        place = 0
        for columns in columns_refs:
            made = lax.dot_general(columns[...], right, FIRST, preferred_element_type=F32)
            first = 0
            while first < made.shape[0]:
                out = grads_out[place]
                out[:, part] = made[first : first + out.shape[0]].astype(out.dtype)
                first += out.shape[0]
                place += 1


def make_softmax(core, counts, lines, early, chunks, per_slot, shapes, scale):
    rows, enc = lines.shape
    late = sum(c.shape[0] for c in chunks)
    keys = early.shape[1] + late
    period = shapes[0][0]
    return pl.pallas_call(
        functools.partial(softmax_kernel, scale, per_slot, period, len(chunks)),
        out_shape=[
            jax.ShapeDtypeStruct((rows // 3, early.shape[1]), BF),
            jax.ShapeDtypeStruct((rows // 3, late), BF),
        ]
        + [jax.ShapeDtypeStruct((n, enc), kind) for n, kind in shapes],
        in_specs=[pl.BlockSpec(memory_space=pltpu.SMEM)] * 2 + in_vmem(2 + len(chunks)),
        out_specs=in_vmem(2 + len(shapes)),
        scratch_shapes=[
            pltpu.VMEM((late, enc), BF),
            pltpu.VMEM((rows, late), F32),
            pltpu.VMEM((rows // 3 * 2, early.shape[1]), BF),
            pltpu.VMEM((rows // 3 * 2, late), BF),
        ],
        compiler_params=pltpu.CompilerParams(vmem_limit_bytes=VMEM_LIMIT),
        cost_estimate=pl.CostEstimate(
            flops=2 * rows * (late + keys) * enc,
            bytes_accessed=2 * enc * (rows + late + 2 * keys) + 4 * rows * keys,
            transcendentals=rows * keys // 2,
        ),
    )(core, counts, lines, early, *chunks)


def attended_kernel(first, second, value_own, value_partner, *refs):
    own, partner, keys, high, low = refs[-5:]
    gather(refs[:-5], keys)
    split, step = first.shape[1], 4 * DH

    @pl.loop(0, keys.shape[1] // step)
    def _(i):
        part = pl.ds(pl.multiple_of(i * step, step), step)
        mixed = dot(first[...], keys[:split, part]) + dot(second[...], keys[split:, part])
        rounded = mixed.astype(BF)
        high[:, part] = rounded
        low[:, part] = (mixed - rounded.astype(F32)).astype(BF)

    length, width = own.shape
    for i, (weight, out) in enumerate(((value_own, own), (value_partner, partner))):
        for h in range(width // DH):
            rows = slice((i * (width // DH) + h) * length, (i * (width // DH) + h + 1) * length)
            part = slice(h * DH, (h + 1) * DH)
            made = dot(high[rows], weight[:, part]) + dot(low[rows], weight[:, part])
            out[:, part] = made.astype(BF)


def make_attended(weights, values, early, late, length):
    rows, enc = weights[0].shape[0], values[0].shape[0]
    keys = weights[0].shape[1] + weights[1].shape[1]
    out = jax.ShapeDtypeStruct((length, values[0].shape[1]), BF)
    return pl.pallas_call(
        attended_kernel,
        out_shape=(out, out),
        in_specs=in_vmem(4 + len(early) + len(late)),
        out_specs=in_vmem(2),
        scratch_shapes=[pltpu.VMEM((n, enc), BF) for n in (keys, rows, rows)],
        compiler_params=pltpu.CompilerParams(vmem_limit_bytes=VMEM_LIMIT),
        cost_estimate=pl.CostEstimate(
            flops=2 * rows * keys * enc, bytes_accessed=2 * keys * (rows + enc), transcendentals=0
        ),
    )(*weights, *values, *early, *late)


def pick_kernel(parts, source, rows, *outs):
    count, _, width = outs[0].shape
    for k in range(parts):

        @pl.loop(0, count)
        def _(i, k=k):
            index = source[k * count + i]
            value = rows[jnp.maximum(index, 0), :, :width]
            outs[k][i] = jnp.where(index >= 0, value, jnp.zeros_like(value))


def join_kernel(core, source, first, second, out):
    split = first.shape[0]

    @pl.loop(0, out.shape[0])
    def _(i):
        slot = jnp.maximum(source[i], 0)
        place = jnp.where(core[0] == 0, slot, (slot + split) % (2 * split))
        low = jnp.minimum(place, split - 1)
        high = jnp.maximum(place - split, 0)
        out[i] = jnp.where(place < split, first[low], second[high])


def join_pick(first, second, source, core):
    shape = (source.shape[0],) + first.shape[1:]
    return pl.pallas_call(
        join_kernel,
        out_shape=jax.ShapeDtypeStruct(shape, BF),
        in_specs=[pl.BlockSpec(memory_space=pltpu.SMEM)] * 2 + in_vmem(2),
        out_specs=in_vmem(1)[0],
        cost_estimate=pl.CostEstimate(
            flops=0, bytes_accessed=4 * math.prod(shape), transcendentals=0
        ),
    )(core, source, first, second)


def pick(rows, source, width=None, parts=1):
    shape = (source.shape[0] // parts, rows.shape[1], width or rows.shape[2])
    return pl.pallas_call(
        functools.partial(pick_kernel, parts),
        out_shape=[jax.ShapeDtypeStruct(shape, BF)] * parts,
        in_specs=[pl.BlockSpec(memory_space=pltpu.SMEM)] + in_vmem(1),
        out_specs=in_vmem(parts),
        cost_estimate=pl.CostEstimate(
            flops=0, bytes_accessed=4 * parts * math.prod(shape), transcendentals=0
        ),
    )(source.astype(jnp.int32), rows)


def pack_kernel(slots_group, owner, rows, hidden, grad, out, position, both, counts):
    both[: hidden.shape[0]] = hidden[...]
    both[hidden.shape[0] :] = grad[...]
    count, height, width = rows.shape
    capacity = count // counts.shape[0]
    out[:, :, width:] = jnp.full((count, height, DH), -1, BF)
    for g in range(counts.shape[0]):
        counts[g] = 0

    @pl.loop(0, count)
    def _(i):
        slot = owner[i]
        position[i] = -1

        @pl.when(slot >= 0)
        def _():
            group = slot // slots_group
            place = group * capacity + counts[group]
            counts[group] += 1
            position[i] = place
            out[place, :, :width] = rows[i]
            tag = (slot - group * slots_group).astype(F32)
            out[place, :, width:] = jnp.full((height, DH), tag).astype(BF)


def pack(rows, hidden, grad, owner, groups, slots_group):
    count, height, width = rows.shape
    return pl.pallas_call(
        functools.partial(pack_kernel, slots_group),
        out_shape=(
            jax.ShapeDtypeStruct((count, height, width + DH), BF),
            jax.ShapeDtypeStruct((count,), jnp.int32),
            jax.ShapeDtypeStruct((2 * hidden.shape[0], hidden.shape[1]), BF),
        ),
        in_specs=[pl.BlockSpec(memory_space=pltpu.SMEM)] + in_vmem(3),
        out_specs=in_vmem(1) + [pl.BlockSpec(memory_space=pltpu.SMEM)] + in_vmem(1),
        scratch_shapes=[pltpu.SMEM((groups,), jnp.int32)],
        cost_estimate=pl.CostEstimate(
            flops=0, bytes_accessed=4 * math.prod(rows.shape), transcendentals=0
        ),
    )(owner, rows, hidden, grad)


def per_device(hidden_in, out_grad, neighbours, counts, slot_owner, w_query, w_key, w_value, w_out):
    groups = lax.axis_size("dp")
    spans = counts.shape[0]
    slots_group = spans * MAXN
    src_slots = slot_owner.shape[0]
    capacity = src_slots // groups
    reach = lax.axis_size("mp") // 4
    rows_dev = neighbours.shape[1]
    enc_width = neighbours.shape[2]
    tokens_dev = hidden_in.shape[0]
    span_len = tokens_dev // spans
    devices = lax.axis_size("mp")
    chips = devices // 2
    core = (lax.axis_index("mp") % 2).astype(jnp.int32)

    slot_order = jnp.arange(src_slots, dtype=jnp.int32)
    send_rows, position, both = pack(
        neighbours, hidden_in, out_grad, slot_owner, groups, slots_group
    )
    both = lax.all_gather(both, "mp", axis=1, tiled=True)
    got = lax.all_to_all(
        send_rows.reshape(groups, capacity, rows_dev, enc_width + DH),
        "dp",
        split_axis=0,
        concat_axis=0,
        tiled=True,
    ).reshape(src_slots, rows_dev, enc_width + DH)
    local_slot = got[:, 0, enc_width].astype(jnp.int32)
    slots = jnp.arange(slots_group, dtype=jnp.int32)
    wanted = (slots + core * MAXN) % slots_group
    matches = local_slot[None, :] == wanted[:, None]
    chosen = jnp.sum(jnp.where(matches, slot_order[None, :] + 1, 0), axis=1) - 1
    chunk_rows = MAXN * rows_dev
    kept, given = pick(got, chosen, enc_width, spans)
    kept, given = kept.reshape(chunk_rows, enc_width), given.reshape(chunk_rows, enc_width)
    given = core_swap(given)
    w_key_partner, w_value_partner = core_swap(w_key), core_swap(w_value)
    queries = dot(both[:tokens_dev], w_query).astype(BF)
    grad_attended = dot_t(both[tokens_dev:], w_out).astype(BF)
    pair = jnp.concatenate([queries, grad_attended], axis=1)
    ups, downs = [kept, given], [kept, given]
    keys = [kept, given]
    for step in range(1, reach):
        ups, downs = ring_step(ups, downs)
        keys += ups + downs
    tokens = [
        lax.dynamic_slice_in_dim(pair, c * span_len, span_len, 0) for c in (core, 1 - core)
    ]
    lines = make_lines(
        tokens[0], core_swap(tokens[1]), (w_key, w_value, w_key_partner, w_value_partner)
    )
    ups[0], downs[1] = after([ups[0], downs[1]], lines)
    keys += [chip_shift(ups[0], 1), chip_shift(downs[1], -1)]
    first_late = 2 + 4 * (reach - 2)
    early, late = keys[:first_late], keys[first_late:]

    shapes = [(chunk_rows, BF)] * len(keys)
    outs = make_softmax(
        core.reshape(1),
        counts,
        lines,
        make_products(lines, early),
        late,
        rows_dev,
        shapes,
        1.0 / math.sqrt(DH),
    )
    weights, grads = outs[:2], outs[2:]
    attended, away = make_attended(weights, (w_value, w_value_partner), early, late, span_len)
    back = core_swap(away)
    attended = jnp.where(
        core == 0,
        jnp.concatenate([attended, back], axis=0),
        jnp.concatenate([back, attended], axis=0),
    )
    mine, other = project_out(core.reshape(1), attended, w_out, chips)
    sums = (mine + core_swap(other)).astype(BF)

    def part(distance, ring):
        return grads[4 * abs(distance) - 2 + (2 if distance > 0 else 0) + ring]

    chains = [
        (0, 1, reach, grads[-2]),
        (1, 1, reach - 1, part(reach - 1, 1)),
        (0, -1, reach - 1, part(1 - reach, 0)),
        (1, -1, reach, grads[-1]),
    ]
    scattered = [grads[0].astype(F32), grads[1].astype(F32)]
    for step in range(reach):
        moved = []
        for ring, way, left, value in chains:
            value = chip_shift(value, way).astype(F32)
            if left > 1:
                value = (value + part(way * (left - 1), ring)).astype(BF)
                moved.append((ring, way, left - 1, value))
            else:
                scattered[ring] = scattered[ring] + value
        chains = moved
    scattered = to_bf16(scattered)
    scattered[1] = core_swap(scattered[1])
    scattered = [part.reshape(MAXN, rows_dev, enc_width) for part in scattered]

    layer_out = lax.psum_scatter(
        sums,
        "mp",
        scatter_dimension=0,
        axis_index_groups=[list(range(c, devices, 2)) for c in range(2)],
    )

    returned = lax.all_to_all(
        join_pick(*scattered, local_slot, core.reshape(1)).reshape(groups, capacity, rows_dev, enc_width),
        "dp",
        split_axis=0,
        concat_axis=0,
        tiled=True,
    ).reshape(src_slots, rows_dev, enc_width)
    neighbour_grad = pick(returned, position)[0]
    return (layer_out, neighbour_grad)


def solution(mesh):
    return jax.shard_map(
        per_device,
        mesh=mesh,
        in_specs=(
            P("dp", "mp"),
            P("dp", "mp"),
            P("dp", "mp", None),
            P("dp"),
            P("dp"),
            P(None, "mp"),
            P(None, "mp"),
            P(None, "mp"),
            P("mp", None),
        ),
        out_specs=(P("dp", "mp"), P("dp", "mp", None)),
        check_vma=False,
    )
```
